256 devices in a mesh: section: 4 (over x_hi, core), cand: 8 (over z), dp: 8 (over x_lo, y).
Axes of the slice: x: 4 (x_hi: 2, x_lo: 2; x = x_hi * 2 + x_lo), y: 4, z: 8, core: 2. Of those that a mesh axis runs over, the one named last changes fastest.
Arguments:
- inputs: bfloat16 [1024, 8192], P('dp', 'cand'), may hold values from -6 to 6
- parent_gain: float32 [4, 8192], P('section'), may hold values from 0.1 to 1.9
- query_weight: bfloat16 [4, 8192, 4096], P('section', 'dp', 'cand'), may hold values from -0.0625 to 0.0625
- key_value_weight: bfloat16 [4, 2, 8192, 512], P('section', None, 'dp'), may hold values from -0.0625 to 0.0625
- output_weight: bfloat16 [4, 4096, 8192], P('section', 'cand', 'dp'), may hold values from -0.09375 to 0.09375
- candidate_gain: float32 [4, 8, 8192], P('section', 'cand'), may hold values from 0.1 to 1.9
- candidate_down: bfloat16 [4, 8, 64, 8192], P('section', 'cand'), may hold values from -0.0625 to 0.0625
- candidate_up: bfloat16 [4, 8, 64, 8192], P('section', 'cand'), may hold values from -0.75 to 0.75
- kept_ranks: int32 [4, 8], P('section', 'cand'), may hold values from 16 to 64
Outputs:
- states: bfloat16 [4, 1024, 8192], P('section', 'dp', 'cand')
- gradient_down: float32 [4, 8, 64, 8192], P('section', 'cand', None, 'dp')
- gradient_up: float32 [4, 8, 64, 8192], P('section', 'cand', None, 'dp')
The draws below stay inside these ranges and needn't reach their ends.
Inputs may be any that keep to these rules, and one draw needn't show every extreme that they name: `kept_ranks`: each candidate keeps at least a quarter of its 64 rank components.
All inputs are finite; a program needn't handle non-finite values.
Results may differ from the reference program's by a relative error of at most 0.025.
Values may be sent and summed in bfloat16 or wider, within the bound.
A program may use at most 128 MiB of HBM per device.

```python
import jax
import jax.numpy as jnp
from jax import lax

D = 8192
HQ = 32
KVH = 4
HD = 128
R = 64
TOK_DEV = 128
TOKENS = 1024
SECTIONS = 4
CANDS = 8
N_SECTION = 4
N_CAND = 8
N_DP = 8


def plant(array, key, least, top_value):
    dims = array.shape
    place = [jax.random.randint(jax.random.fold_in(key, axis), (), 0, dims[axis]) for axis in range(len(dims))]
    array = array.at[tuple(place)].set(least)
    longest = dims.index(max(dims))
    place[longest] = (place[longest] + 1) % dims[longest]
    return array.at[tuple(place)].set(top_value)


def block_scale(stream_key, extent, pieces, low, high):
    gain, own = 1.0, jax.random.fold_in(stream_key, 6)
    for axis_at, blocks in pieces:
        draws = jnp.exp(jax.random.uniform(jax.random.fold_in(own, axis_at), (blocks,), jnp.float32, low / len(pieces), high / len(pieces)))
        gain = gain * jnp.repeat(draws, extent[axis_at] // blocks).reshape([-1 if axis == axis_at else 1 for axis in range(len(extent))])
    return gain


def centred(rng, extent, width, limit, split=(), kind=jnp.bfloat16):
    loudness = block_scale(rng, extent, split, -0.22, 0.18) if split else 1.0
    entries = jax.random.normal(rng, extent, jnp.float32) * width * loudness
    return jnp.minimum(jnp.maximum(entries, -limit), limit).astype(kind)


def setup_inputs(seed: int = 0) -> dict:
    arg_keys = jax.random.split(jax.random.key(seed), 10)
    return {
        "inputs": centred(arg_keys[0], (TOKENS, D), 1.0, 6.0, ((0, 8), (1, 8))),
        "parent_gain": jnp.clip(1.0 + 0.18 * jax.random.normal(arg_keys[1], (SECTIONS, D), jnp.float32), 0.1, 1.9),
        "query_weight": centred(arg_keys[2], (SECTIONS, D, HQ * HD), D ** -0.5, 0.0625, ((0, 4), (1, 8), (2, 8))),
        "key_value_weight": centred(arg_keys[3], (SECTIONS, 2, D, KVH * HD), D ** -0.5, 0.0625, ((0, 4), (2, 8))),
        "output_weight": centred(arg_keys[4], (SECTIONS, HQ * HD, D), (HQ * HD) ** -0.5, 0.09375, ((0, 4), (1, 8), (2, 8))),
        "candidate_gain": jnp.clip(1.0 + 0.18 * jax.random.normal(arg_keys[5], (SECTIONS, CANDS, D), jnp.float32), 0.1, 1.9),
        "candidate_down": centred(arg_keys[6], (SECTIONS, CANDS, R, D), D ** -0.5, 0.0625, ((0, 4), (1, 8))),
        "candidate_up": centred(arg_keys[7], (SECTIONS, CANDS, R, D), R ** -0.5, 0.75, ((0, 4), (1, 8))),
        "kept_ranks": plant(jax.random.randint(arg_keys[8], (SECTIONS, CANDS), R // 4, R + 1), jax.random.fold_in(arg_keys[8], 1), R // 4, R).astype(jnp.int32),
    }


epsilon = 1e-05
rope_base = 500000.0

def rotate(matrix, positions):
    half_size = matrix.shape[-1] // 2
    frequency = rope_base ** (-jnp.arange(half_size, dtype=jnp.float32) / half_size)
    angles = positions.astype(jnp.float32)[:, None] * frequency[None, :]
    cosine = jnp.cos(angles)[:, None, :]
    sine_part = jnp.sin(angles)[:, None, :]
    lower_half = matrix[..., :half_size]
    upper_half = matrix[..., half_size:]
    return jnp.concatenate([lower_half * cosine - upper_half * sine_part, upper_half * cosine + lower_half * sine_part], axis=-1)

def normed(values, gain_row):
    wide = values.astype(jnp.float32)
    inverse_rms = lax.rsqrt(lax.optimization_barrier(jnp.mean(wide * wide, axis=-1, keepdims=True)) + epsilon)
    return (wide * inverse_rms * gain_row.astype(jnp.float32)).astype(jnp.bfloat16)

def attend_sequence(operands):
    queries, key_rows, value_rows = operands
    grouped = queries.astype(jnp.float32).reshape(TOK_DEV, KVH, HQ // KVH, HD)
    scores = jnp.einsum('qkgd,skd->kgqs', grouped, key_rows.astype(jnp.float32), precision=lax.Precision.HIGHEST) * HD ** (-0.5)
    positions = jnp.arange(TOK_DEV)
    allowed = positions[None, :] <= positions[:, None]
    weights_exp = jnp.where(allowed, jnp.exp(scores), 0.0)
    weights = (weights_exp / lax.optimization_barrier(jnp.sum(weights_exp, axis=-1, keepdims=True))).astype(jnp.bfloat16)
    mixed = jnp.einsum('kgqs,skd->qkgd', weights.astype(jnp.float32), value_rows.astype(jnp.float32), precision=lax.Precision.HIGHEST)
    return mixed.astype(jnp.bfloat16).reshape(TOK_DEV, HQ * HD)

def candidate_terms(features, produced, gain_row, down_rows, up_rows, rank_mask):
    cnormed = normed(features, gain_row)
    hidden = (jnp.dot(cnormed, down_rows.T, preferred_element_type=jnp.float32) * rank_mask).astype(jnp.bfloat16)
    branch = jnp.dot(hidden, up_rows, preferred_element_type=jnp.float32)
    difference = branch - (produced.astype(jnp.float32) - features.astype(jnp.float32))
    scaled = (difference / TOKENS).astype(jnp.bfloat16)
    gradient_up = jnp.dot(hidden.T, scaled, preferred_element_type=jnp.float32)
    backward = (jnp.dot(scaled, up_rows.T, preferred_element_type=jnp.float32) * rank_mask).astype(jnp.bfloat16)
    gradient_down = jnp.dot(backward.T, cnormed, preferred_element_type=jnp.float32)
    return (gradient_down, gradient_up)

def reference(inputs, parent_gain, query_weight, key_value_weight, output_weight, candidate_gain, candidate_down, candidate_up, kept_ranks):
    positions = jnp.tile(jnp.arange(TOK_DEV), N_DP)
    group_heads = HQ // N_CAND
    current = inputs
    state_list = []
    down_list = []
    up_list = []
    for section_index in range(N_SECTION):
        normalized = normed(current, parent_gain[section_index])
        queries = jnp.dot(normalized, query_weight[section_index], preferred_element_type=jnp.float32).reshape(TOKENS, HQ, HD)
        queries = rotate(queries, positions).astype(jnp.bfloat16)
        key_rows = jnp.dot(normalized, key_value_weight[section_index, 0], preferred_element_type=jnp.float32).reshape(TOKENS, KVH, HD)
        key_rows = rotate(key_rows, positions).astype(jnp.bfloat16)
        value_rows = jnp.dot(normalized, key_value_weight[section_index, 1], preferred_element_type=jnp.float32).astype(jnp.bfloat16).reshape(TOKENS, KVH, HD)
        attended = lax.map(attend_sequence, (queries.reshape(N_DP, TOK_DEV, HQ, HD), key_rows.reshape(N_DP, TOK_DEV, KVH, HD), value_rows.reshape(N_DP, TOK_DEV, KVH, HD)))
        attended = attended.reshape(TOKENS, HQ * HD)
        summed = jnp.zeros((TOKENS, D), jnp.float32)
        for group_index in range(N_CAND):
            lower = group_index * group_heads * HD
            upper = lower + group_heads * HD
            group_part = jnp.dot(attended[:, lower:upper], output_weight[section_index, lower:upper], preferred_element_type=jnp.float32)
            summed = summed + lax.optimization_barrier(group_part.astype(jnp.bfloat16)).astype(jnp.float32)
        produced = (current.astype(jnp.float32) + summed).astype(jnp.bfloat16)
        state_list.append(produced)
        section_down = []
        section_up = []
        for candidate in range(N_CAND):
            rank_mask = (jnp.arange(R) < kept_ranks[section_index, candidate]).astype(jnp.float32)
            gradient_down, gradient_up = candidate_terms(current, produced, candidate_gain[section_index, candidate], candidate_down[section_index, candidate], candidate_up[section_index, candidate], rank_mask)
            section_down.append(gradient_down)
            section_up.append(gradient_up)
        down_list.append(jnp.stack(section_down))
        up_list.append(jnp.stack(section_up))
        current = produced
    return (jnp.stack(state_list), jnp.stack(down_list), jnp.stack(up_list))
```

```python
import functools

import jax
import jax.numpy as jnp
import numpy as np
from jax import lax
from jax.experimental import pallas as pl
from jax.experimental.pallas import tpu as pltpu
from jax.sharding import PartitionSpec as P

HD = 128
LANES = 128
EPSILON = 1e-05
ROPE_BASE = 500000.0
MESH = pl.DeviceIdType.MESH
F32 = jnp.float32
BF16 = jnp.bfloat16


def dot_nt(a, b):
    return lax.dot_general(a, b, (((1,), (1,)), ((), ())), preferred_element_type=F32)


def dot_tn(a, b):
    return lax.dot_general(a, b, (((0,), (0,)), ((), ())), preferred_element_type=F32)


def rope_tables(tokens):
    half = HD // 2
    frequency = (ROPE_BASE ** (-np.arange(half, dtype=np.float64) / half)).astype(np.float32)
    angles = np.arange(tokens, dtype=np.float32)[:, None] * frequency[None, :]
    angles = angles.astype(np.float64)
    cosine, sine = np.cos(angles), np.sin(angles)
    full_cos = np.concatenate([cosine, cosine], axis=1).astype(np.float32)
    full_sin = np.concatenate([-sine, sine], axis=1).astype(np.float32)
    return full_cos, full_sin


def body(
    N,
    S,
    sharing,
    inputs,
    parent_gain,
    query_weight,
    key_value_weight,
    output_weight,
    candidate_gain,
    candidate_down,
    candidate_up,
    kept,
    cos_table,
    sin_table,
    states_out,
    down_out,
    up_out,
    x_buf,
    st_buf,
    sc_buf,
    p_buf,
    r_buf,
    a_own,
    a_buf,
    s_send,
    s_recv,
    part,
    w_qkv,
    w_out,
    w_down,
    w_up,
    pg,
    cg,
    cos_v,
    sin_v,
    bw_send,
    bw_recv,
    bw_all,
    y_buf,
    g_down,
    g_up,
    load_sem,
    in_send,
    in_recv,
    nx_send,
    nx_recv,
    ag_send,
    ag_recv,
    sg_send,
    sg_recv,
    p_send,
    p_recv,
    a_send,
    a_recv,
    rs_send,
    rs_recv,
    mate_send,
    mate_recv,
    y_send,
    y_recv,
    b_send,
    b_recv,
    c_send,
    c_recv,
):
    s = lax.axis_index("section")
    z = lax.axis_index("cand")
    i = lax.axis_index("dp")
    T, F = inputs.shape
    R = candidate_down.shape[2]
    D = N * F
    QW = query_weight.shape[2]
    heads = QW // HD
    KW = QW + 2 * HD
    piece = T // N
    half_rows = T // 2
    token_total = T * N
    middle = N // 2

    def wrap(index):
        return lax.rem(index + 2 * N, N)

    def rows(index):
        return pl.ds(pl.multiple_of(index * piece, piece), piece)

    def remote(source, target, send, recv, **device):
        return pltpu.make_async_remote_copy(
            src_ref=source,
            dst_ref=target,
            send_sem=send,
            recv_sem=recv,
            device_id=device,
            device_id_type=MESH,
        )

    def wait_bytes(ref, sem):
        pltpu.make_async_copy(ref, ref, sem).wait()

    features = pl.ds(pl.multiple_of(i * F, F), F)
    kv_columns = pl.ds(pl.multiple_of((z // sharing) * HD, HD), HD)
    loads = [
        (query_weight.at[0], w_qkv.at[:, pl.ds(0, QW)]),
        (key_value_weight.at[0, 0, :, kv_columns], w_qkv.at[:, pl.ds(QW, HD)]),
        (key_value_weight.at[0, 1, :, kv_columns], w_qkv.at[:, pl.ds(QW + HD, HD)]),
        (output_weight.at[0], w_out),
        (candidate_down.at[0, 0, :, features], w_down.at[pl.ds(0, R)]),
        (candidate_up.at[0, 0, :, features], w_up.at[pl.ds(0, R)]),
        (parent_gain.at[:, features], pg),
        (candidate_gain.at[0, :, features], cg),
        (cos_table, cos_v),
        (sin_table, sin_v),
    ]
    copies = [
        pltpu.make_async_copy(source, target, load_sem.at[k])
        for k, (source, target) in enumerate(loads)
    ]
    for copy in copies:
        copy.start()

    barrier = pltpu.get_barrier_semaphore()

    def greet(**device):
        pl.semaphore_signal(barrier, inc=1, device_id=device, device_id_type=MESH)

    diagonal = i == z
    greet(cand=wrap(z + 1))
    greet(cand=wrap(z - 1))
    for k in range(1, N):
        greet(dp=wrap(i + k))
    for w in range(N):

        @pl.when(jnp.logical_not(diagonal & (z == w)))
        def _(w=w):
            greet(dp=z, cand=w)
            greet(dp=w, cand=i)

    @pl.when(s > 0)
    def _():
        greet(section=s - 1)

    @pl.when(s < S - 1)
    def _():
        greet(section=s + 1)

    expected = (
        2
        + (N - 1)
        + 2 * N
        - 2 * diagonal.astype(jnp.int32)
        + (s > 0).astype(jnp.int32)
        + (s < S - 1).astype(jnp.int32)
    )
    pl.semaphore_wait(barrier, expected)

    def input_piece(w):
        source = inputs.at[pl.ds(w * piece, piece)]
        target = x_buf.at[w, rows(i)]
        return source, target

    @pl.when(s == 0)
    def _():
        for w in range(N):
            source, target = input_piece(w)
            own = diagonal & (z == w)

            @pl.when(own)
            def _(source=source, target=target):
                pltpu.make_async_copy(source, target, in_recv.at[0]).start()

            @pl.when(jnp.logical_not(own))
            def _(source=source, target=target, w=w):
                remote(source, target, in_send.at[w], in_recv.at[0], dp=z, cand=w).start()

    for copy in copies:
        copy.wait()
    w_down[pl.ds(R, LANES - R), :] = jnp.zeros((LANES - R, F), BF16)
    w_up[pl.ds(R, LANES - R), :] = jnp.zeros((LANES - R, F), BF16)
    w_down[pl.ds(0, R), :] = (w_down[pl.ds(0, R), :].astype(F32) * cg[...]).astype(BF16)

    def half(index):
        return pl.ds(index * half_rows, half_rows)

    def link(buffer, block, h, way, k, send, recv):
        place = buffer.at[block, half(h)]
        return remote(
            place, place, send.at[way, k], recv.at[way, k], cand=wrap(z + 1 - 2 * way)
        )

    def gather_own(buffer, h, send, recv):
        link(buffer, z, h, 0, h, send, recv).start()
        link(buffer, z, h, 1, 1 - h, send, recv).start()

    def gathered(k, way):
        distance = k // 2 + 1
        block = wrap(z - distance + 2 * distance * way)
        h = k % 2 if way == 0 else 1 - k % 2
        return block, h

    def gather_step(buffer, k, send, recv):
        for way in (0, 1):
            block, h = gathered(k, way)
            wait_bytes(buffer.at[block, half(h)], recv.at[way, k])
            if k + 2 <= N - 2:
                link(buffer, block, h, way, k + 2, send, recv).start()

    def gather_finish(buffer, send):
        for way in (0, 1):
            for k in range(N - 1):
                wait_bytes(buffer.at[0, half(0)], send.at[way, k])

    lane = lax.broadcasted_iota(jnp.int32, (T, LANES), 1)

    def project(block):
        values = x_buf[block]
        wide = values.astype(F32)
        scaled = (wide * pg[...]).astype(BF16)
        p_buf[block, :, pl.ds(0, KW)] = jnp.dot(
            scaled, w_qkv[...], preferred_element_type=F32
        ).astype(BF16)
        hidden = dot_nt(values, w_down[...])
        squares = jnp.sum(wide * wide, axis=-1, keepdims=True)
        coarse = squares.astype(BF16).astype(F32)
        extra = jnp.where(lane == R, coarse, jnp.where(lane == R + 1, squares - coarse, hidden))
        p_buf[block, :, pl.ds(KW, LANES)] = extra.astype(BF16)
        for k in range(1, N):
            t = wrap(i + k)
            remote(
                p_buf.at[block, rows(t)],
                r_buf.at[i, rows(block)],
                p_send.at[k],
                p_recv.at[k],
                dp=t,
            ).start()
        r_buf[i, rows(block), :] = p_buf[block, rows(i), :]

    @pl.when(s == 0)
    def _():
        wait_bytes(x_buf.at[z], in_recv.at[0])

    for h in (0, 1):

        @pl.when(s > 0)
        def _(h=h):
            wait_bytes(x_buf.at[z, half(h)], nx_recv.at[h])

        gather_own(x_buf, h, ag_send, ag_recv)
    project(z)
    for j in range(middle - 1):
        gather_step(x_buf, 2 * j, ag_send, ag_recv)
        gather_step(x_buf, 2 * j + 1, ag_send, ag_recv)
        project(wrap(z - j - 1))
        project(wrap(z + j + 1))
    gather_step(x_buf, N - 2, ag_send, ag_recv)
    project(wrap(z + middle))

    odd = lax.rem(s, 2) == 1

    def mate_copy(d):
        place = x_buf.at[wrap(z + d)]
        return remote(
            place, st_buf.at[wrap(z + d)], mate_send.at[d], mate_recv.at[d], section=s - 1
        )

    for k in range(1, N):
        wait_bytes(r_buf.at[wrap(i - k)], p_recv.at[k])

    def summed(b):
        total = r_buf[0, :, pl.ds(b * LANES, LANES)].astype(F32)
        for source in range(1, N):
            total += r_buf[source, :, pl.ds(b * LANES, LANES)].astype(F32)
        return total

    extra = summed(heads + 2)
    squares = extra[:, R : R + 1] + extra[:, R + 1 : R + 2]
    inverse = lax.rsqrt(squares / D + EPSILON)
    keep = (lax.broadcasted_iota(jnp.int32, (1, LANES), 1) < kept[0, 0]).astype(F32)
    hidden = extra * inverse * keep
    inverse_coarse = inverse.astype(BF16).astype(F32)
    a_own[:, pl.ds(QW, LANES)] = jnp.where(
        lane == R, inverse_coarse, jnp.where(lane == R + 1, inverse - inverse_coarse, hidden)
    ).astype(BF16)

    def rotated(matrix):
        return (matrix * cos_v[...] + pltpu.roll(matrix, HD // 2, 1) * sin_v[...]).astype(BF16)

    keys = rotated(summed(heads) * inverse)
    values = (summed(heads + 1) * inverse).astype(BF16)
    allowed = lax.broadcasted_iota(jnp.int32, (T, T), 1) <= lax.broadcasted_iota(
        jnp.int32, (T, T), 0
    )
    for h in range(heads):
        queries = rotated(summed(h) * inverse)
        scores = dot_nt(queries, keys) * HD ** (-0.5)
        raised = jnp.where(allowed, jnp.exp(scores), 0.0)
        weights = (raised / jnp.sum(raised, axis=-1, keepdims=True)).astype(BF16)
        a_own[:, pl.ds(h * HD, HD)] = jnp.dot(
            weights, values, preferred_element_type=F32
        ).astype(BF16)

    offsets = [middle]
    for m in range(middle - 1, 0, -1):
        offsets += [m, -m]
    offsets.append(0)
    for d, offset in enumerate(offsets):
        block = wrap(z + offset)
        for k in range(1, N):
            remote(
                a_own.at[rows(block)],
                a_buf.at[block, rows(i)],
                a_send.at[d],
                a_recv.at[d],
                dp=wrap(i + k),
            ).start()
        a_buf[block, rows(i), :] = a_own[rows(block), :]

    @pl.when(odd)
    def _():
        for d in range(1, N):
            mate_copy(d).start()

    def project_out(offset):
        d = offsets.index(offset)
        block = wrap(z + offset)
        wait_bytes(a_buf.at[block, pl.ds(0, T - piece)], a_recv.at[d])
        return jnp.dot(a_buf[block, :, pl.ds(0, QW)], w_out[...], preferred_element_type=F32)

    def emit(way, k, value):
        s_send[way, k] = value.astype(BF16)
        remote(
            s_send.at[way, k],
            s_recv.at[way, k],
            rs_send.at[way, k],
            rs_recv.at[way, k],
            cand=wrap(z + 1 - 2 * way),
        ).start()

    def got(way, k):
        wait_bytes(s_recv.at[way, k], rs_recv.at[way, k])
        return s_recv[way, k].astype(F32)

    first, second = half(0), half(1)
    part[0] = project_out(middle)
    emit(0, 0, part[0, first])
    emit(1, 0, part[0, second])
    for j, m in enumerate(range(middle - 1, 0, -1)):
        part[0] = project_out(m)
        part[1] = project_out(-m)
        if j == 0:
            emit(0, 1, part[0, second])
            emit(1, 1, part[1, first])
        else:
            emit(0, 2 * j + 1, got(0, 2 * j - 1) + part[0, second])
            emit(1, 2 * j + 1, got(1, 2 * j - 1) + part[1, first])
        emit(0, 2 * j + 2, got(0, 2 * j) + part[0, first])
        emit(1, 2 * j + 2, got(1, 2 * j) + part[1, second])
    part[0] = project_out(0)

    def next_copy(h):
        return remote(
            st_buf.at[z, half(h)], x_buf.at[z, half(h)], nx_send.at[h], nx_recv.at[h], section=s + 1
        )

    for h in (0, 1):
        update = part[0, half(h)] + got(0, N - 2 - h) + got(1, N - 3 + h)
        st_buf[z, half(h), :] = (x_buf[z, half(h), :].astype(F32) + update).astype(BF16)

        @pl.when(s < S - 1)
        def _(h=h):
            next_copy(h).start()

        @pl.when(odd)
        def _(h=h):
            gather_own(st_buf, h, sg_send, sg_recv)

    def state_piece(t):
        source = st_buf.at[z, pl.ds(t * piece, piece)]
        target = y_buf.at[rows(z)]
        return source, target

    for t in range(N):
        source, target = state_piece(t)
        own = diagonal & (i == t)

        @pl.when(own)
        def _(source=source, target=target):
            pltpu.make_async_copy(source, target, y_recv.at[0]).start()

        @pl.when(jnp.logical_not(own))
        def _(source=source, target=target, t=t):
            remote(source, target, y_send.at[t], y_recv.at[0], dp=t, cand=i).start()

    def candidate(block):
        hidden = a_buf[block, :, pl.ds(QW, LANES)]
        branch = jnp.dot(hidden, w_up[...], preferred_element_type=F32)
        difference = branch - (st_buf[block].astype(F32) - x_buf[block].astype(F32))
        scaled = (difference * (1.0 / token_total)).astype(BF16)
        sc_buf[block] = scaled
        backward = dot_nt(scaled, w_up[...]).astype(BF16)
        bw_send[block] = backward

        @pl.when(block == i)
        def _():
            bw_recv[i] = bw_send[block]

        @pl.when(block != i)
        def _():
            remote(
                bw_send.at[block], bw_recv.at[i], b_send.at[block], b_recv.at[0], dp=block
            ).start()

    candidate(z)
    for j in range(middle):
        last = j == middle - 1

        @pl.when(odd)
        def _(j=j, last=last):
            gather_step(st_buf, 2 * j, sg_send, sg_recv)
            if not last:
                gather_step(st_buf, 2 * j + 1, sg_send, sg_recv)

        @pl.when(jnp.logical_not(odd))
        def _(j=j, last=last):
            wait_bytes(st_buf.at[wrap(z + j + 1)], mate_recv.at[j + 1])
            if not last:
                wait_bytes(st_buf.at[wrap(z - j - 1)], mate_recv.at[N - j - 1])

        candidate(wrap(z + j + 1))
        if not last:
            candidate(wrap(z - j - 1))

    wait_bytes(bw_recv.at[pl.ds(0, N - 1)], b_recv.at[0])
    backward = bw_recv[0].astype(F32)
    for source in range(1, N):
        backward += bw_recv[source].astype(F32)
    own_extra = a_buf[i, :, pl.ds(QW, LANES)].astype(F32)
    own_inverse = own_extra[:, R : R + 1] + own_extra[:, R + 1 : R + 2]
    bw_all[i] = (backward * keep * own_inverse).astype(BF16)

    def spread(k):
        return remote(
            bw_all.at[i], bw_all.at[i], c_send.at[k], c_recv.at[0], dp=wrap(i + k)
        )

    for k in range(1, N):
        spread(k).start()

    hidden_all = a_buf[:, :, pl.ds(QW, LANES)].reshape(N * T, LANES)
    g_up[...] = dot_tn(hidden_all, sc_buf[...].reshape(N * T, F))
    up_copy = pltpu.make_async_copy(g_up.at[pl.ds(0, R)], up_out.at[0, 0], load_sem.at[0])
    up_copy.start()
    wait_bytes(y_buf, y_recv.at[0])
    y_copy = pltpu.make_async_copy(y_buf, states_out.at[0], load_sem.at[1])
    y_copy.start()

    wait_bytes(bw_all.at[pl.ds(0, N - 1)], c_recv.at[0])
    g_down[...] = (
        dot_tn(bw_all[...].reshape(N * T, LANES), x_buf[...].reshape(N * T, F)) * cg[...]
    )
    down_copy = pltpu.make_async_copy(g_down.at[pl.ds(0, R)], down_out.at[0, 0], load_sem.at[2])
    down_copy.start()

    @pl.when(s == 0)
    def _():
        for w in range(N):

            @pl.when(jnp.logical_not(diagonal & (z == w)))
            def _(w=w):
                wait_bytes(y_buf.at[pl.ds(0, piece)], in_send.at[w])

    gather_finish(x_buf, ag_send)
    for k in range(1, N):
        wait_bytes(r_buf.at[0], p_send.at[k])
        wait_bytes(bw_all.at[0], c_send.at[k])
    for d in range(N):
        wait_bytes(a_buf.at[0, pl.ds(0, T - piece)], a_send.at[d])
    for way in (0, 1):
        for k in range(N - 1):
            wait_bytes(s_send.at[way, k], rs_send.at[way, k])

    @pl.when(s < S - 1)
    def _():
        for h in (0, 1):
            wait_bytes(x_buf.at[0, half(h)], nx_send.at[h])

    @pl.when(odd)
    def _():
        gather_finish(st_buf, sg_send)
        for d in range(1, N):
            wait_bytes(x_buf.at[0], mate_send.at[d])

    for t in range(N):

        @pl.when(jnp.logical_not(diagonal & (i == t)))
        def _(t=t):
            wait_bytes(y_buf.at[pl.ds(0, piece)], y_send.at[t])

        @pl.when(i != t)
        def _(t=t):
            wait_bytes(bw_send.at[0], b_send.at[t])

    up_copy.wait()
    y_copy.wait()
    down_copy.wait()


def shards(
    inputs,
    parent_gain,
    query_weight,
    key_value_weight,
    output_weight,
    candidate_gain,
    candidate_down,
    candidate_up,
    kept_ranks,
):
    N = lax.axis_size("cand")
    S = lax.axis_size("section")
    T, F = inputs.shape
    R = candidate_down.shape[2]
    QW = query_weight.shape[2]
    KW = QW + 2 * HD
    half_rows = T // 2
    sharing = N // (key_value_weight.shape[3] // HD)
    cos_table, sin_table = rope_tables(T)
    anywhere = pl.BlockSpec(memory_space=pl.ANY)
    dma = pltpu.SemaphoreType.DMA
    return pl.pallas_call(
        functools.partial(body, N, S, sharing),
        out_shape=(
            jax.ShapeDtypeStruct((1, T, F), BF16),
            jax.ShapeDtypeStruct((1, 1, R, F), F32),
            jax.ShapeDtypeStruct((1, 1, R, F), F32),
        ),
        in_specs=[anywhere] * 8 + [pl.BlockSpec(memory_space=pltpu.SMEM)] + [anywhere] * 2,
        out_specs=(anywhere,) * 3,
        scratch_shapes=[
            pltpu.VMEM((N, T, F), BF16),
            pltpu.VMEM((N, T, F), BF16),
            pltpu.VMEM((N, T, F), BF16),
            pltpu.VMEM((N, T, KW + LANES), BF16),
            pltpu.VMEM((N, T, KW + LANES), BF16),
            pltpu.VMEM((T, QW + LANES), BF16),
            pltpu.VMEM((N, T, QW + LANES), BF16),
            pltpu.VMEM((2, N - 1, half_rows, F), BF16),
            pltpu.VMEM((2, N - 1, half_rows, F), BF16),
            pltpu.VMEM((2, T, F), F32),
            pltpu.VMEM((F, KW), BF16),
            pltpu.VMEM((QW, F), BF16),
            pltpu.VMEM((LANES, F), BF16),
            pltpu.VMEM((LANES, F), BF16),
            pltpu.VMEM((1, F), F32),
            pltpu.VMEM((1, F), F32),
            pltpu.VMEM((T, HD), F32),
            pltpu.VMEM((T, HD), F32),
            pltpu.VMEM((N, T, LANES), BF16),
            pltpu.VMEM((N, T, LANES), BF16),
            pltpu.VMEM((N, T, LANES), BF16),
            pltpu.VMEM((T, F), BF16),
            pltpu.VMEM((LANES, F), F32),
            pltpu.VMEM((LANES, F), F32),
            dma((10,)),
            dma((N,)),
            dma((1,)),
            dma((2,)),
            dma((2,)),
            dma((2, N - 1)),
            dma((2, N - 1)),
            dma((2, N - 1)),
            dma((2, N - 1)),
            dma((N,)),
            dma((N,)),
            dma((N,)),
            dma((N,)),
            dma((2, N - 1)),
            dma((2, N - 1)),
            dma((N,)),
            dma((N,)),
            dma((N,)),
            dma((1,)),
            dma((N,)),
            dma((1,)),
            dma((N,)),
            dma((1,)),
        ],
        compiler_params=pltpu.CompilerParams(
            collective_id=0, has_side_effects=True, vmem_limit_bytes=40 * 1024 * 1024
        ),
    )(
        inputs,
        parent_gain,
        query_weight,
        key_value_weight,
        output_weight,
        candidate_gain,
        candidate_down,
        candidate_up,
        kept_ranks,
        jnp.asarray(cos_table),
        jnp.asarray(sin_table),
    )


def solution(mesh):
    placed = (
        P("dp", "cand"),
        P("section", None),
        P("section", "dp", "cand"),
        P("section", None, "dp", None),
        P("section", "cand", "dp"),
        P("section", "cand", None),
        P("section", "cand", None, None),
        P("section", "cand", None, None),
        P("section", "cand"),
    )
    return jax.shard_map(
        shards,
        mesh=mesh,
        in_specs=placed,
        out_specs=(
            P("section", "dp", "cand"),
            P("section", "cand", None, "dp"),
            P("section", "cand", None, "dp"),
        ),
        check_vma=False,
    )
```

```python
import functools

import jax
import jax.numpy as jnp
import numpy as np
from jax import lax
from jax.experimental import pallas as pl
from jax.experimental.pallas import tpu as pltpu
from jax.sharding import PartitionSpec as P

HD = 128
LANES = 128
PIECES = 4
EPSILON = 1e-05
ROPE_BASE = 500000.0
MESH = pl.DeviceIdType.MESH
F32 = jnp.float32
BF16 = jnp.bfloat16


def dot_nt(a, b):
    return lax.dot_general(a, b, (((1,), (1,)), ((), ())), preferred_element_type=F32)


def dot_tn(a, b):
    return lax.dot_general(a, b, (((0,), (0,)), ((), ())), preferred_element_type=F32)


def rope_tables(tokens):
    half = HD // 2
    frequency = (ROPE_BASE ** (-np.arange(half, dtype=np.float64) / half)).astype(np.float32)
    angles = np.arange(tokens, dtype=np.float32)[:, None] * frequency[None, :]
    angles = angles.astype(np.float64)
    cosine, sine = np.cos(angles), np.sin(angles)
    full_cos = np.concatenate([cosine, cosine], axis=1).astype(np.float32)
    full_sin = np.concatenate([-sine, sine], axis=1).astype(np.float32)
    return full_cos, full_sin


def body(
    N,
    S,
    sharing,
    inputs,
    parent_gain,
    query_weight,
    key_value_weight,
    output_weight,
    candidate_gain,
    candidate_down,
    candidate_up,
    kept,
    cos_table,
    sin_table,
    states_out,
    down_out,
    up_out,
    x_buf,
    st_buf,
    sc_buf,
    p_buf,
    r_buf,
    a_own,
    a_buf,
    s_send,
    s_recv,
    part,
    w_qkv,
    w_out,
    w_down,
    w_up,
    pg,
    cg,
    cos_v,
    sin_v,
    bw_send,
    bw_recv,
    bw_all,
    y_buf,
    g_down,
    g_up,
    load_sem,
    in_send,
    in_recv,
    nx_send,
    nx_recv,
    ag_send,
    ag_recv,
    sg_send,
    sg_recv,
    p_send,
    p_recv,
    a_send,
    a_recv,
    rs_send,
    rs_recv,
    mate_send,
    mate_recv,
    y_send,
    y_recv,
    b_send,
    b_recv,
    c_send,
    c_recv,
):
    s = lax.axis_index("section")
    z = lax.axis_index("cand")
    i = lax.axis_index("dp")
    T, F = inputs.shape
    R = candidate_down.shape[2]
    D = N * F
    QW = query_weight.shape[2]
    heads = QW // HD
    KW = QW + 2 * HD
    piece = T // N
    token_total = T * N
    middle = N // 2

    def wrap(index):
        return lax.rem(index + 2 * N, N)

    def rows(index):
        return pl.ds(pl.multiple_of(index * piece, piece), piece)

    def remote(source, target, send, recv, **device):
        return pltpu.make_async_remote_copy(
            src_ref=source,
            dst_ref=target,
            send_sem=send,
            recv_sem=recv,
            device_id=device,
            device_id_type=MESH,
        )

    def wait_bytes(ref, sem):
        pltpu.make_async_copy(ref, ref, sem).wait()

    features = pl.ds(pl.multiple_of(i * F, F), F)
    kv_columns = pl.ds(pl.multiple_of((z // sharing) * HD, HD), HD)
    loads = [
        (query_weight.at[0], w_qkv.at[:, pl.ds(0, QW)]),
        (key_value_weight.at[0, 0, :, kv_columns], w_qkv.at[:, pl.ds(QW, HD)]),
        (key_value_weight.at[0, 1, :, kv_columns], w_qkv.at[:, pl.ds(QW + HD, HD)]),
        (output_weight.at[0], w_out),
        (candidate_down.at[0, 0, :, features], w_down.at[pl.ds(0, R)]),
        (candidate_up.at[0, 0, :, features], w_up.at[pl.ds(0, R)]),
        (parent_gain.at[:, features], pg),
        (candidate_gain.at[0, :, features], cg),
        (cos_table, cos_v),
        (sin_table, sin_v),
    ]
    copies = [
        pltpu.make_async_copy(source, target, load_sem.at[k])
        for k, (source, target) in enumerate(loads)
    ]
    for copy in copies:
        copy.start()

    barrier = pltpu.get_barrier_semaphore()

    def greet(**device):
        pl.semaphore_signal(barrier, inc=1, device_id=device, device_id_type=MESH)

    diagonal = i == z
    odd = lax.rem(s, 2) == 1
    greet(cand=wrap(z + 1))
    greet(cand=wrap(z - 1))
    for k in range(1, N):
        greet(dp=wrap(i + k))
    for w in range(N):

        @pl.when(jnp.logical_not(diagonal & (z == w)))
        def _(w=w):
            greet(dp=z, cand=w)
            greet(dp=w, cand=i)

    @pl.when(s > 0)
    def _():
        greet(section=s - 1)

    @pl.when(s < S - 1)
    def _():
        greet(section=s + 1)

    mate = s + 1 - 2 * lax.rem(s, 2)
    greet(section=mate, cand=wrap(z + 1))
    greet(section=mate, cand=wrap(z - 1))

    expected = (
        4
        + (N - 1)
        + 2 * N
        - 2 * diagonal.astype(jnp.int32)
        + (s > 0).astype(jnp.int32)
        + (s < S - 1).astype(jnp.int32)
    )
    pl.semaphore_wait(barrier, expected)

    pieces = PIECES
    messages = (N - 1) * pieces // 2
    piece_rows = T // pieces

    def part_rows(q):
        return pl.ds(q * piece_rows, piece_rows)

    def piece_of(way, k):
        return k % pieces if way == 0 else pieces - 1 - k % pieces

    def toward(way):
        return wrap(z + 1 - 2 * way)

    def send_input():
        for w in range(N):
            source = inputs.at[pl.ds(w * piece, piece)]
            target = x_buf.at[w, rows(i)]
            own = diagonal & (z == w)

            @pl.when(own)
            def _(source=source, target=target):
                pltpu.make_async_copy(source, target, in_recv.at[0]).start()

            @pl.when(jnp.logical_not(own))
            def _(source=source, target=target, w=w):
                remote(source, target, in_send.at[0], in_recv.at[0], dp=z, cand=w).start()

    def wait_pieces_sent(sem):
        @pl.when(diagonal)
        def _():
            wait_bytes(y_buf.at[pl.ds(0, T - piece)], sem)

        @pl.when(jnp.logical_not(diagonal))
        def _():
            wait_bytes(y_buf, sem)

    def prepare():
        for copy in copies:
            copy.wait()
        w_down[pl.ds(R, LANES - R), :] = jnp.zeros((LANES - R, F), BF16)
        w_up[pl.ds(R, LANES - R), :] = jnp.zeros((LANES - R, F), BF16)
        w_down[pl.ds(0, R), :] = (w_down[pl.ds(0, R), :].astype(F32) * cg[...]).astype(BF16)

    def forward(buffer, block, way, k, send, recv):
        place = buffer.at[block, part_rows(piece_of(way, k))]
        remote(place, place, send.at[0], recv.at[way, k], cand=toward(way)).start()

    def gather_step(buffer, k, send, recv):
        distance = k // pieces + 1
        for way in (0, 1):
            block = wrap(z - distance + 2 * distance * way)
            wait_bytes(buffer.at[block, part_rows(piece_of(way, k))], recv.at[way, k])
            if k + pieces < messages:
                forward(buffer, block, way, k + pieces, send, recv)

    lane = lax.broadcasted_iota(jnp.int32, (T, LANES), 1)
    keep = (lax.broadcasted_iota(jnp.int32, (1, LANES), 1) < kept[0, 0]).astype(F32)

    def project(block):
        values = x_buf[block]
        wide = values.astype(F32)
        scaled = (wide * pg[...]).astype(BF16)
        p_buf[block, :, pl.ds(0, KW)] = jnp.dot(
            scaled, w_qkv[...], preferred_element_type=F32
        ).astype(BF16)
        hidden = dot_nt(values, w_down[...])
        squares = jnp.sum(wide * wide, axis=-1, keepdims=True)
        coarse = squares.astype(BF16).astype(F32)
        extra = jnp.where(lane == R, coarse, jnp.where(lane == R + 1, squares - coarse, hidden))
        p_buf[block, :, pl.ds(KW, LANES)] = extra.astype(BF16)
        for k in range(1, N):
            t = wrap(i + k)
            remote(
                p_buf.at[block, rows(t)],
                r_buf.at[i, rows(block)],
                p_send.at[0],
                p_recv.at[0],
                dp=t,
            ).start()
        r_buf[i, rows(block), :] = p_buf[block, rows(i), :]

    def gather_and_project():
        @pl.when(s == 0)
        def _():
            wait_bytes(x_buf.at[z], in_recv.at[0])

        for q in range(pieces):

            @pl.when(s > 0)
            def _(q=q):
                wait_bytes(x_buf.at[z, part_rows(q)], nx_recv.at[q])

            @pl.when(jnp.logical_not(odd))
            def _(q=q):
                forward(x_buf, z, 0, q, ag_send, ag_recv)
                forward(x_buf, z, 1, pieces - 1 - q, ag_send, ag_recv)

        project(z)
        for j in range(middle):
            for k in range(j * pieces, min((j + 1) * pieces, messages)):
                gather_step(x_buf, k, ag_send, ag_recv)
            project(wrap(z + j + 1))
            if j < middle - 1:
                project(wrap(z - j - 1))

    def summed(b):
        total = r_buf[0, :, pl.ds(b * LANES, LANES)].astype(F32)
        for source in range(1, N):
            total += r_buf[source, :, pl.ds(b * LANES, LANES)].astype(F32)
        return total

    def rotated(matrix):
        return (matrix * cos_v[...] + pltpu.roll(matrix, HD // 2, 1) * sin_v[...]).astype(BF16)

    offsets = [middle]
    for m in range(middle - 1, 0, -1):
        offsets += [m, -m]
    offsets.append(0)

    def attention():
        wait_bytes(r_buf.at[pl.ds(0, N - 1)], p_recv.at[0])
        extra = summed(heads + 2)
        squares = extra[:, R : R + 1] + extra[:, R + 1 : R + 2]
        inverse = lax.rsqrt(squares / D + EPSILON)
        hidden = extra * inverse * keep
        inverse_coarse = inverse.astype(BF16).astype(F32)
        a_own[:, pl.ds(QW, LANES)] = jnp.where(
            lane == R, inverse_coarse, jnp.where(lane == R + 1, inverse - inverse_coarse, hidden)
        ).astype(BF16)
        keys = rotated(summed(heads) * inverse)
        values = (summed(heads + 1) * inverse).astype(BF16)
        allowed = lax.broadcasted_iota(jnp.int32, (T, T), 1) <= lax.broadcasted_iota(
            jnp.int32, (T, T), 0
        )
        for h in range(heads):
            queries = rotated(summed(h) * inverse)
            scores = dot_nt(queries, keys) * HD ** (-0.5)
            raised = jnp.where(allowed, jnp.exp(scores), 0.0)
            weights = (raised / jnp.sum(raised, axis=-1, keepdims=True)).astype(BF16)
            a_own[:, pl.ds(h * HD, HD)] = jnp.dot(
                weights, values, preferred_element_type=F32
            ).astype(BF16)
        for d, offset in enumerate(offsets):
            block = wrap(z + offset)
            for k in range(1, N):
                remote(
                    a_own.at[rows(block)],
                    a_buf.at[block, rows(i)],
                    a_send.at[0],
                    a_recv.at[d],
                    dp=wrap(i + k),
                ).start()
            a_buf[block, rows(i), :] = a_own[rows(block), :]

    def project_out(slot, offset):
        block = wrap(z + offset)
        wait_bytes(a_buf.at[block, pl.ds(0, T - piece)], a_recv.at[offsets.index(offset)])
        part[slot] = jnp.dot(
            a_buf[block, :, pl.ds(0, QW)], w_out[...], preferred_element_type=F32
        )

    def got(way, k):
        wait_bytes(s_recv.at[way, k], rs_recv.at[way, k])
        return s_recv[way, k].astype(F32)

    def emit(slot, way, k):
        value = part[slot, part_rows(piece_of(way, k)), :]
        if k >= pieces:
            value += got(way, k - pieces)
        s_send[way, k] = value.astype(BF16)
        remote(
            s_send.at[way, k],
            s_recv.at[way, k],
            rs_send.at[0],
            rs_recv.at[way, k],
            cand=toward(way),
        ).start()

    def output():
        project_out(0, middle)
        for k in range(pieces // 2):
            emit(0, 0, k)
            emit(0, 1, k)
        for j, m in enumerate(range(middle - 1, 0, -1)):
            project_out(0, m)
            project_out(1, -m)
            for k in range(pieces // 2 + j * pieces, pieces // 2 + (j + 1) * pieces):
                emit(0, 0, k)
                emit(1, 1, k)
        project_out(0, 0)
        part[0] += x_buf[z].astype(F32)
        for k in range(messages - pieces, messages):
            for way in (0, 1):
                place = part_rows(piece_of(way, k))
                total = part[0, place, :] + got(way, k)
                part[0, place, :] = total

    def hand_over():
        st_buf[z] = part[0].astype(BF16)

        @pl.when(jnp.logical_not(odd))
        def _():
            for k in range(pieces):
                for way in (0, 1):
                    place = part_rows(piece_of(way, k))
                    remote(
                        st_buf.at[z, place],
                        x_buf.at[z, place],
                        nx_send.at[0],
                        ag_recv.at[way, k],
                        section=s + 1,
                        cand=toward(way),
                    ).start()

        @pl.when(s < S - 1)
        def _():
            for q in range(pieces):
                remote(
                    st_buf.at[z, part_rows(q)],
                    x_buf.at[z, part_rows(q)],
                    nx_send.at[0],
                    nx_recv.at[q],
                    section=s + 1,
                ).start()

        @pl.when(odd)
        def _():
            for q in range(pieces):
                forward(st_buf, z, 0, q, sg_send, sg_recv)
                forward(st_buf, z, 1, pieces - 1 - q, sg_send, sg_recv)
            for d in range(1, N):
                place = x_buf.at[wrap(z + d)]
                remote(
                    place,
                    st_buf.at[wrap(z + d)],
                    mate_send.at[0],
                    mate_recv.at[d],
                    section=s - 1,
                ).start()

        for t in range(N):
            source = st_buf.at[z, pl.ds(t * piece, piece)]
            target = y_buf.at[rows(z)]
            own = diagonal & (i == t)

            @pl.when(own)
            def _(source=source, target=target):
                pltpu.make_async_copy(source, target, y_recv.at[0]).start()

            @pl.when(jnp.logical_not(own))
            def _(source=source, target=target, t=t):
                remote(source, target, y_send.at[0], y_recv.at[0], dp=t, cand=i).start()

    def candidate(block):
        hidden = a_buf[block, :, pl.ds(QW, LANES)]
        branch = jnp.dot(hidden, w_up[...], preferred_element_type=F32)
        difference = branch - (st_buf[block].astype(F32) - x_buf[block].astype(F32))
        scaled = (difference * (1.0 / token_total)).astype(BF16)
        sc_buf[block] = scaled
        bw_send[block] = dot_nt(scaled, w_up[...]).astype(BF16)

        @pl.when(block == i)
        def _():
            bw_recv[i] = bw_send[block]

        @pl.when(block != i)
        def _():
            remote(
                bw_send.at[block], bw_recv.at[i], b_send.at[0], b_recv.at[0], dp=block
            ).start()

    def candidates():
        candidate(z)
        for j in range(middle):
            last = j == middle - 1

            @pl.when(odd)
            def _(j=j):
                for k in range(j * pieces, min((j + 1) * pieces, messages)):
                    gather_step(st_buf, k, sg_send, sg_recv)

            @pl.when(jnp.logical_not(odd))
            def _(j=j, last=last):
                wait_bytes(st_buf.at[wrap(z + j + 1)], mate_recv.at[j + 1])
                if not last:
                    wait_bytes(st_buf.at[wrap(z - j - 1)], mate_recv.at[N - j - 1])

            candidate(wrap(z + j + 1))
            if not last:
                candidate(wrap(z - j - 1))

    def gradients():
        wait_bytes(bw_recv.at[pl.ds(0, N - 1)], b_recv.at[0])
        backward = bw_recv[0].astype(F32)
        for source in range(1, N):
            backward += bw_recv[source].astype(F32)
        own_extra = a_buf[i, :, pl.ds(QW, LANES)].astype(F32)
        own_inverse = own_extra[:, R : R + 1] + own_extra[:, R + 1 : R + 2]
        bw_all[i] = (backward * keep * own_inverse).astype(BF16)
        for k in range(1, N):
            remote(
                bw_all.at[i], bw_all.at[i], c_send.at[0], c_recv.at[0], dp=wrap(i + k)
            ).start()

        hidden_all = a_buf[:, :, pl.ds(QW, LANES)].reshape(N * T, LANES)
        g_up[...] = dot_tn(hidden_all, sc_buf[...].reshape(N * T, F))
        up_copy = pltpu.make_async_copy(g_up.at[pl.ds(0, R)], up_out.at[0, 0], load_sem.at[0])
        up_copy.start()
        wait_bytes(y_buf, y_recv.at[0])
        y_copy = pltpu.make_async_copy(y_buf, states_out.at[0], load_sem.at[1])
        y_copy.start()

        wait_bytes(bw_all.at[pl.ds(0, N - 1)], c_recv.at[0])
        g_down[...] = (
            dot_tn(bw_all[...].reshape(N * T, LANES), x_buf[...].reshape(N * T, F)) * cg[...]
        )
        down_copy = pltpu.make_async_copy(
            g_down.at[pl.ds(0, R)], down_out.at[0, 0], load_sem.at[2]
        )
        down_copy.start()
        up_copy.wait()
        y_copy.wait()
        down_copy.wait()

    def drain():
        @pl.when(s == 0)
        def _():
            wait_pieces_sent(in_send.at[0])

        others = pl.ds(0, N - 1)

        @pl.when(jnp.logical_not(odd))
        def _():
            wait_bytes(x_buf.at[others], ag_send.at[0])
            wait_bytes(x_buf.at[pl.ds(0, 3)], nx_send.at[0])

        @pl.when(odd)
        def _():
            wait_bytes(x_buf.at[pl.ds(0, N - 3)], ag_send.at[0])
            wait_bytes(st_buf.at[others], sg_send.at[0])
            wait_bytes(st_buf.at[others], mate_send.at[0])

            @pl.when(s < S - 1)
            def _():
                wait_bytes(x_buf.at[0], nx_send.at[0])

        wait_bytes(p_buf.at[others], p_send.at[0])
        wait_bytes(a_buf.at[others], a_send.at[0])
        wait_bytes(s_send, rs_send.at[0])
        wait_pieces_sent(y_send.at[0])
        wait_bytes(bw_send.at[others], b_send.at[0])
        wait_bytes(bw_all.at[others], c_send.at[0])

    @pl.when(s == 0)
    def _():
        send_input()

    prepare()
    gather_and_project()
    attention()
    output()
    hand_over()
    candidates()
    gradients()
    drain()


def shards(
    inputs,
    parent_gain,
    query_weight,
    key_value_weight,
    output_weight,
    candidate_gain,
    candidate_down,
    candidate_up,
    kept_ranks,
):
    N = lax.axis_size("cand")
    S = lax.axis_size("section")
    T, F = inputs.shape
    R = candidate_down.shape[2]
    QW = query_weight.shape[2]
    KW = QW + 2 * HD
    pieces = PIECES
    messages = (N - 1) * pieces // 2
    sharing = N // (key_value_weight.shape[3] // HD)
    cos_table, sin_table = rope_tables(T)
    anywhere = pl.BlockSpec(memory_space=pl.ANY)
    dma = pltpu.SemaphoreType.DMA
    return pl.pallas_call(
        functools.partial(body, N, S, sharing),
        out_shape=(
            jax.ShapeDtypeStruct((1, T, F), BF16),
            jax.ShapeDtypeStruct((1, 1, R, F), F32),
            jax.ShapeDtypeStruct((1, 1, R, F), F32),
        ),
        in_specs=[anywhere] * 8 + [pl.BlockSpec(memory_space=pltpu.SMEM)] + [anywhere] * 2,
        out_specs=(anywhere,) * 3,
        scratch_shapes=[
            pltpu.VMEM((N, T, F), BF16),
            pltpu.VMEM((N, T, F), BF16),
            pltpu.VMEM((N, T, F), BF16),
            pltpu.VMEM((N, T, KW + LANES), BF16),
            pltpu.VMEM((N, T, KW + LANES), BF16),
            pltpu.VMEM((T, QW + LANES), BF16),
            pltpu.VMEM((N, T, QW + LANES), BF16),
            pltpu.VMEM((2, messages, T // pieces, F), BF16),
            pltpu.VMEM((2, messages, T // pieces, F), BF16),
            pltpu.VMEM((2, T, F), F32),
            pltpu.VMEM((F, KW), BF16),
            pltpu.VMEM((QW, F), BF16),
            pltpu.VMEM((LANES, F), BF16),
            pltpu.VMEM((LANES, F), BF16),
            pltpu.VMEM((1, F), F32),
            pltpu.VMEM((1, F), F32),
            pltpu.VMEM((T, HD), F32),
            pltpu.VMEM((T, HD), F32),
            pltpu.VMEM((N, T, LANES), BF16),
            pltpu.VMEM((N, T, LANES), BF16),
            pltpu.VMEM((N, T, LANES), BF16),
            pltpu.VMEM((T, F), BF16),
            pltpu.VMEM((LANES, F), F32),
            pltpu.VMEM((LANES, F), F32),
            dma((10,)),
            dma((1,)),
            dma((1,)),
            dma((1,)),
            dma((pieces,)),
            dma((1,)),
            dma((2, messages)),
            dma((1,)),
            dma((2, messages)),
            dma((1,)),
            dma((1,)),
            dma((1,)),
            dma((N,)),
            dma((1,)),
            dma((2, messages)),
            dma((1,)),
            dma((N,)),
            dma((1,)),
            dma((1,)),
            dma((1,)),
            dma((1,)),
            dma((1,)),
            dma((1,)),
        ],
        compiler_params=pltpu.CompilerParams(
            collective_id=0, has_side_effects=True, vmem_limit_bytes=56 * 1024 * 1024
        ),
    )(
        inputs,
        parent_gain,
        query_weight,
        key_value_weight,
        output_weight,
        candidate_gain,
        candidate_down,
        candidate_up,
        kept_ranks,
        jnp.asarray(cos_table),
        jnp.asarray(sin_table),
    )


def solution(mesh):
    placed = (
        P("dp", "cand"),
        P("section", None),
        P("section", "dp", "cand"),
        P("section", None, "dp", None),
        P("section", "cand", "dp"),
        P("section", "cand", None),
        P("section", "cand", None, None),
        P("section", "cand", None, None),
        P("section", "cand"),
    )
    return jax.shard_map(
        shards,
        mesh=mesh,
        in_specs=placed,
        out_specs=(
            P("section", "dp", "cand"),
            P("section", "cand", None, "dp"),
            P("section", "cand", None, "dp"),
        ),
        check_vma=False,
    )
```

```python
import functools

import jax
import jax.numpy as jnp
import numpy as np
from jax import lax
from jax.experimental import pallas as pl
from jax.experimental.pallas import tpu as pltpu
from jax.sharding import PartitionSpec as P

HD = 128
LANES = 128
PIECES = 4
EPSILON = 1e-05
ROPE_BASE = 500000.0
MESH = pl.DeviceIdType.MESH
F32 = jnp.float32
BF16 = jnp.bfloat16


def dot_nt(a, b):
    return lax.dot_general(a, b, (((1,), (1,)), ((), ())), preferred_element_type=F32)


def dot_tn(a, b):
    return lax.dot_general(a, b, (((0,), (0,)), ((), ())), preferred_element_type=F32)


def rope_tables(tokens):
    half = HD // 2
    frequency = (ROPE_BASE ** (-np.arange(half, dtype=np.float64) / half)).astype(np.float32)
    angles = np.arange(tokens, dtype=np.float32)[:, None] * frequency[None, :]
    angles = angles.astype(np.float64)
    cosine, sine = np.cos(angles), np.sin(angles)
    full_cos = np.concatenate([cosine, cosine], axis=1).astype(np.float32)
    full_sin = np.concatenate([-sine, sine], axis=1).astype(np.float32)
    return full_cos, full_sin


def body(
    N,
    S,
    sharing,
    inputs,
    parent_gain,
    query_weight,
    key_value_weight,
    output_weight,
    candidate_gain,
    candidate_down,
    candidate_up,
    kept,
    cos_table,
    sin_table,
    states_out,
    down_out,
    up_out,
    x_buf,
    st_buf,
    sc_buf,
    p_buf,
    r_buf,
    a_own,
    a_buf,
    s_send,
    s_recv,
    part,
    w_qkv,
    w_out,
    w_down,
    w_up,
    pg,
    cg,
    cos_v,
    sin_v,
    bw_send,
    bw_recv,
    bw_all,
    y_buf,
    g_down,
    g_up,
    load_sem,
    in_send,
    in_recv,
    nx_send,
    nx_recv,
    ag_send,
    ag_recv,
    sg_send,
    sg_recv,
    p_send,
    p_recv,
    a_send,
    a_recv,
    rs_send,
    rs_recv,
    mate_send,
    mate_recv,
    y_send,
    y_recv,
    b_send,
    b_recv,
    c_send,
    c_recv,
):
    s = lax.axis_index("section")
    z = lax.axis_index("cand")
    i = lax.axis_index("dp")
    T, F = inputs.shape
    R = candidate_down.shape[2]
    D = N * F
    QW = query_weight.shape[2]
    heads = QW // HD
    KW = QW + 2 * HD
    piece = T // N
    token_total = T * N
    middle = N // 2

    def wrap(index):
        return lax.rem(index + 2 * N, N)

    def rows(index):
        return pl.ds(pl.multiple_of(index * piece, piece), piece)

    def remote(source, target, send, recv, **device):
        return pltpu.make_async_remote_copy(
            src_ref=source,
            dst_ref=target,
            send_sem=send,
            recv_sem=recv,
            device_id=device,
            device_id_type=MESH,
        )

    def wait_bytes(ref, sem):
        pltpu.make_async_copy(ref, ref, sem).wait()

    features = pl.ds(pl.multiple_of(i * F, F), F)
    kv_columns = pl.ds(pl.multiple_of((z // sharing) * HD, HD), HD)
    loads = [
        (query_weight.at[0], w_qkv.at[:, pl.ds(0, QW)]),
        (key_value_weight.at[0, 0, :, kv_columns], w_qkv.at[:, pl.ds(QW, HD)]),
        (key_value_weight.at[0, 1, :, kv_columns], w_qkv.at[:, pl.ds(QW + HD, HD)]),
        (output_weight.at[0], w_out),
        (candidate_down.at[0, 0, :, features], w_down.at[pl.ds(0, R)]),
        (candidate_up.at[0, 0, :, features], w_up.at[pl.ds(0, R)]),
        (parent_gain.at[:, features], pg),
        (candidate_gain.at[0, :, features], cg),
        (cos_table, cos_v),
        (sin_table, sin_v),
    ]
    copies = [
        pltpu.make_async_copy(source, target, load_sem.at[k])
        for k, (source, target) in enumerate(loads)
    ]
    for copy in copies:
        copy.start()

    barrier = pltpu.get_barrier_semaphore()

    def greet(**device):
        pl.semaphore_signal(barrier, inc=1, device_id=device, device_id_type=MESH)

    diagonal = i == z
    odd = lax.rem(s, 2) == 1
    greet(cand=wrap(z + 1))
    greet(cand=wrap(z - 1))
    for k in range(1, N):
        greet(dp=wrap(i + k))
    for w in range(N):

        @pl.when(jnp.logical_not(diagonal & (z == w)))
        def _(w=w):
            greet(dp=z, cand=w)
            greet(dp=w, cand=i)

    @pl.when(s > 0)
    def _():
        greet(section=s - 1)

    @pl.when(s < S - 1)
    def _():
        greet(section=s + 1)

    mate = s + 1 - 2 * lax.rem(s, 2)
    greet(section=mate, cand=wrap(z + 1))
    greet(section=mate, cand=wrap(z - 1))

    expected = (
        4
        + (N - 1)
        + 2 * N
        - 2 * diagonal.astype(jnp.int32)
        + (s > 0).astype(jnp.int32)
        + (s < S - 1).astype(jnp.int32)
    )
    pl.semaphore_wait(barrier, expected)

    pieces = PIECES
    messages = (N - 1) * pieces // 2
    piece_rows = T // pieces

    def part_rows(q):
        return pl.ds(q * piece_rows, piece_rows)

    def piece_of(way, k):
        return k % pieces if way == 0 else pieces - 1 - k % pieces

    def toward(way):
        return wrap(z + 1 - 2 * way)

    def send_input():
        for w in range(N):
            source = inputs.at[pl.ds(w * piece, piece)]
            target = x_buf.at[w, rows(i)]
            own = diagonal & (z == w)

            @pl.when(own)
            def _(source=source, target=target):
                pltpu.make_async_copy(source, target, in_recv.at[0]).start()

            @pl.when(jnp.logical_not(own))
            def _(source=source, target=target, w=w):
                remote(source, target, in_send.at[0], in_recv.at[0], dp=z, cand=w).start()

    def wait_pieces_sent(sem):
        @pl.when(diagonal)
        def _():
            wait_bytes(y_buf.at[pl.ds(0, T - piece)], sem)

        @pl.when(jnp.logical_not(diagonal))
        def _():
            wait_bytes(y_buf, sem)

    def prepare():
        for copy in copies:
            copy.wait()
        w_down[pl.ds(R, LANES - R), :] = jnp.zeros((LANES - R, F), BF16)
        w_up[pl.ds(R, LANES - R), :] = jnp.zeros((LANES - R, F), BF16)
        w_down[pl.ds(0, R), :] = (w_down[pl.ds(0, R), :].astype(F32) * cg[...]).astype(BF16)

    def relay(source, target, block, distance, way, k, send, recv, **device):
        place = part_rows(piece_of(way, k))
        if distance < middle - 1 or (distance == middle - 1 and k < pieces // 2):
            remote(
                source.at[block, place],
                target.at[block, place],
                send.at[0],
                recv.at[way, distance * pieces + k],
                cand=toward(way),
                **device,
            ).start()

    def gather_step(buffer, k, send, recv):
        distance = k // pieces + 1
        for way in (0, 1):
            block = wrap(z - distance + 2 * distance * way)
            wait_bytes(buffer.at[block, part_rows(piece_of(way, k))], recv.at[way, k])
            relay(buffer, buffer, block, distance, way, k % pieces, send, recv)

    start_order = []
    for q in range(pieces // 2):
        start_order += [q, pieces - 1 - q]
    ready = []
    for n in range(pieces):
        done = set(start_order[: n + 1])
        fresh = []
        for way in (0, 1):
            for k in range(pieces):
                before = all(piece_of(way, b) in done for b in range(k + 1))
                if before and not any((way, k) in earlier for earlier in ready):
                    fresh.append((way, k))
        ready.append(fresh)

    def relay_ready(buffer, n, send, recv):
        for way, k in ready[n]:
            relay(buffer, buffer, z, 0, way, k, send, recv)

    lane = lax.broadcasted_iota(jnp.int32, (T, LANES), 1)
    keep = (lax.broadcasted_iota(jnp.int32, (1, LANES), 1) < kept[0, 0]).astype(F32)

    def project(block):
        values = x_buf[block]
        wide = values.astype(F32)
        scaled = (wide * pg[...]).astype(BF16)
        p_buf[block, :, pl.ds(0, KW)] = jnp.dot(
            scaled, w_qkv[...], preferred_element_type=F32
        ).astype(BF16)
        hidden = dot_nt(values, w_down[...])
        squares = jnp.sum(wide * wide, axis=-1, keepdims=True)
        coarse = squares.astype(BF16).astype(F32)
        extra = jnp.where(lane == R, coarse, jnp.where(lane == R + 1, squares - coarse, hidden))
        p_buf[block, :, pl.ds(KW, LANES)] = extra.astype(BF16)
        for k in range(1, N):
            t = wrap(i + k)
            remote(
                p_buf.at[block, rows(t)],
                r_buf.at[i, rows(block)],
                p_send.at[0],
                p_recv.at[0],
                dp=t,
            ).start()
        r_buf[i, rows(block), :] = p_buf[block, rows(i), :]

    def gather_and_project():
        @pl.when(s == 0)
        def _():
            wait_bytes(x_buf.at[z], in_recv.at[0])

        for n, q in enumerate(start_order):

            @pl.when(s > 0)
            def _(q=q):
                wait_bytes(x_buf.at[z, part_rows(q)], nx_recv.at[q])

            @pl.when(jnp.logical_not(odd))
            def _(n=n):
                relay_ready(x_buf, n, ag_send, ag_recv)

        project(z)
        for j in range(middle):
            for k in range(j * pieces, min((j + 1) * pieces, messages)):
                gather_step(x_buf, k, ag_send, ag_recv)
            project(wrap(z + j + 1))
            if j < middle - 1:
                project(wrap(z - j - 1))

    def summed(b):
        total = r_buf[0, :, pl.ds(b * LANES, LANES)].astype(F32)
        for source in range(1, N):
            total += r_buf[source, :, pl.ds(b * LANES, LANES)].astype(F32)
        return total

    def rotated(matrix):
        return (matrix * cos_v[...] + pltpu.roll(matrix, HD // 2, 1) * sin_v[...]).astype(BF16)

    offsets = [middle]
    for m in range(middle - 1, 0, -1):
        offsets += [m, -m]
    offsets.append(0)

    def attention():
        wait_bytes(r_buf.at[pl.ds(0, N - 1)], p_recv.at[0])
        extra = summed(heads + 2)
        squares = extra[:, R : R + 1] + extra[:, R + 1 : R + 2]
        inverse = lax.rsqrt(squares / D + EPSILON)
        hidden = extra * inverse * keep
        inverse_coarse = inverse.astype(BF16).astype(F32)
        a_own[:, pl.ds(QW, LANES)] = jnp.where(
            lane == R, inverse_coarse, jnp.where(lane == R + 1, inverse - inverse_coarse, hidden)
        ).astype(BF16)
        keys = rotated(summed(heads) * inverse)
        values = (summed(heads + 1) * inverse).astype(BF16)
        allowed = lax.broadcasted_iota(jnp.int32, (T, T), 1) <= lax.broadcasted_iota(
            jnp.int32, (T, T), 0
        )
        for h in range(heads):
            queries = rotated(summed(h) * inverse)
            scores = dot_nt(queries, keys) * HD ** (-0.5)
            raised = jnp.where(allowed, jnp.exp(scores), 0.0)
            weights = (raised / jnp.sum(raised, axis=-1, keepdims=True)).astype(BF16)
            a_own[:, pl.ds(h * HD, HD)] = jnp.dot(
                weights, values, preferred_element_type=F32
            ).astype(BF16)
        for d, offset in enumerate(offsets):
            block = wrap(z + offset)
            for k in range(1, N):
                remote(
                    a_own.at[rows(block)],
                    a_buf.at[block, rows(i)],
                    a_send.at[0],
                    a_recv.at[d],
                    dp=wrap(i + k),
                ).start()
            a_buf[block, rows(i), :] = a_own[rows(block), :]

    def project_out(slot, offset):
        block = wrap(z + offset)
        wait_bytes(a_buf.at[block, pl.ds(0, T - piece)], a_recv.at[offsets.index(offset)])
        part[slot] = jnp.dot(
            a_buf[block, :, pl.ds(0, QW)], w_out[...], preferred_element_type=F32
        )

    def got(way, k):
        wait_bytes(s_recv.at[way, k], rs_recv.at[way, k])
        return s_recv[way, k].astype(F32)

    def slot_of(offset, k):
        return pieces // 2 + (middle - 1 - offset) * pieces + k

    def contribution(offset, way, k):
        if offset < middle - 1:
            return got(way, slot_of(offset + 1, k))
        return got(way, k) if k < pieces // 2 else 0.0

    def emit(way, slot, value):
        s_send[way, slot] = value.astype(BF16)
        remote(
            s_send.at[way, slot],
            s_recv.at[way, slot],
            rs_send.at[0],
            rs_recv.at[way, slot],
            cand=toward(way),
        ).start()

    arrival_order = list(range(pieces // 2, pieces)) + list(range(pieces // 2))

    def mate_copies():
        for d in range(1, N):
            place = wrap(z + d)
            remote(
                x_buf.at[place], st_buf.at[place], mate_send.at[0], mate_recv.at[d], section=s - 1
            ).start()

    def output():
        project_out(0, middle)
        for k in range(pieces // 2):
            for way in (0, 1):
                emit(way, k, part[0, part_rows(piece_of(way, k)), :])
        for m in range(middle - 1, 0, -1):
            project_out(0, m)
            project_out(1, -m)
            for k in arrival_order:
                for way in (0, 1):
                    value = part[way, part_rows(piece_of(way, k)), :]
                    emit(way, slot_of(m, k), value + contribution(m, way, k))
        project_out(0, 0)
        part[0] += x_buf[z].astype(F32)
        for k in arrival_order:
            for way in (0, 1):
                place = part_rows(piece_of(way, k))
                total = part[0, place, :] + contribution(0, way, k)
                part[0, place, :] = total

    def hand_over():
        st_buf[z] = part[0].astype(BF16)

        @pl.when(jnp.logical_not(odd))
        def _():
            for k in range(pieces):
                for way in (0, 1):
                    relay(st_buf, x_buf, z, 0, way, k, nx_send, ag_recv, section=s + 1)

        @pl.when(s < S - 1)
        def _():
            for q in start_order:
                remote(
                    st_buf.at[z, part_rows(q)],
                    x_buf.at[z, part_rows(q)],
                    nx_send.at[0],
                    nx_recv.at[q],
                    section=s + 1,
                ).start()

        @pl.when(odd)
        def _():
            @pl.when(s < S - 1)
            def _():
                wait_bytes(x_buf.at[0], nx_send.at[0])

            for k in range(pieces):
                for way in (0, 1):
                    relay(st_buf, st_buf, z, 0, way, k, sg_send, sg_recv)

        pl.when(odd)(mate_copies)

    def send_state():
        for t in range(N):
            source = st_buf.at[z, pl.ds(t * piece, piece)]
            target = y_buf.at[rows(z)]
            own = diagonal & (i == t)

            @pl.when(own)
            def _(source=source, target=target):
                pltpu.make_async_copy(source, target, y_recv.at[0]).start()

            @pl.when(jnp.logical_not(own))
            def _(source=source, target=target, t=t):
                remote(source, target, y_send.at[0], y_recv.at[0], dp=t, cand=i).start()

    def candidate(block):
        hidden = a_buf[block, :, pl.ds(QW, LANES)]
        branch = jnp.dot(hidden, w_up[...], preferred_element_type=F32)
        difference = branch - (st_buf[block].astype(F32) - x_buf[block].astype(F32))
        scaled = (difference * (1.0 / token_total)).astype(BF16)
        sc_buf[block] = scaled
        bw_send[block] = dot_nt(scaled, w_up[...]).astype(BF16)

        @pl.when(block == i)
        def _():
            bw_recv[i] = bw_send[block]

        @pl.when(block != i)
        def _():
            remote(
                bw_send.at[block], bw_recv.at[i], b_send.at[0], b_recv.at[0], dp=block
            ).start()

    def candidates():
        candidate(z)
        for j in range(middle):
            last = j == middle - 1

            @pl.when(odd)
            def _(j=j):
                for k in range(j * pieces, min((j + 1) * pieces, messages)):
                    gather_step(st_buf, k, sg_send, sg_recv)
                if j == middle - 2:
                    send_state()

            @pl.when(jnp.logical_not(odd))
            def _(j=j, last=last):
                wait_bytes(st_buf.at[wrap(z + j + 1)], mate_recv.at[j + 1])
                if not last:
                    wait_bytes(st_buf.at[wrap(z - j - 1)], mate_recv.at[N - j - 1])

            candidate(wrap(z + j + 1))
            if not last:
                candidate(wrap(z - j - 1))


    def gradients():
        wait_bytes(bw_recv.at[pl.ds(0, N - 1)], b_recv.at[0])
        backward = bw_recv[0].astype(F32)
        for source in range(1, N):
            backward += bw_recv[source].astype(F32)
        own_extra = a_buf[i, :, pl.ds(QW, LANES)].astype(F32)
        own_inverse = own_extra[:, R : R + 1] + own_extra[:, R + 1 : R + 2]
        bw_all[i] = (backward * keep * own_inverse).astype(BF16)
        for k in range(1, N):
            remote(
                bw_all.at[i], bw_all.at[i], c_send.at[0], c_recv.at[0], dp=wrap(i + k)
            ).start()

        hidden_all = a_buf[:, :, pl.ds(QW, LANES)].reshape(N * T, LANES)
        g_up[...] = dot_tn(hidden_all, sc_buf[...].reshape(N * T, F))
        up_copy = pltpu.make_async_copy(g_up.at[pl.ds(0, R)], up_out.at[0, 0], load_sem.at[0])
        up_copy.start()
        pl.when(jnp.logical_not(odd))(send_state)
        wait_bytes(y_buf, y_recv.at[0])
        y_copy = pltpu.make_async_copy(y_buf, states_out.at[0], load_sem.at[1])
        y_copy.start()

        wait_bytes(bw_all.at[pl.ds(0, N - 1)], c_recv.at[0])
        g_down[...] = (
            dot_tn(bw_all[...].reshape(N * T, LANES), x_buf[...].reshape(N * T, F)) * cg[...]
        )
        down_copy = pltpu.make_async_copy(
            g_down.at[pl.ds(0, R)], down_out.at[0, 0], load_sem.at[2]
        )
        down_copy.start()
        up_copy.wait()
        y_copy.wait()
        down_copy.wait()

    def drain():
        @pl.when(s == 0)
        def _():
            wait_pieces_sent(in_send.at[0])

        others = pl.ds(0, N - 1)

        @pl.when(jnp.logical_not(odd))
        def _():
            wait_bytes(x_buf.at[others], ag_send.at[0])
            wait_bytes(x_buf.at[pl.ds(0, 3)], nx_send.at[0])

        @pl.when(odd)
        def _():
            wait_bytes(x_buf.at[pl.ds(0, N - 3)], ag_send.at[0])
            wait_bytes(st_buf.at[others], sg_send.at[0])
            wait_bytes(st_buf.at[others], mate_send.at[0])

        wait_bytes(p_buf.at[others], p_send.at[0])
        wait_bytes(a_buf.at[others], a_send.at[0])
        wait_bytes(s_send, rs_send.at[0])
        wait_pieces_sent(y_send.at[0])
        wait_bytes(bw_send.at[others], b_send.at[0])
        wait_bytes(bw_all.at[others], c_send.at[0])

    @pl.when(s == 0)
    def _():
        send_input()

    prepare()
    gather_and_project()
    attention()
    output()
    hand_over()
    candidates()
    gradients()
    drain()


def shards(
    inputs,
    parent_gain,
    query_weight,
    key_value_weight,
    output_weight,
    candidate_gain,
    candidate_down,
    candidate_up,
    kept_ranks,
):
    N = lax.axis_size("cand")
    S = lax.axis_size("section")
    T, F = inputs.shape
    R = candidate_down.shape[2]
    QW = query_weight.shape[2]
    KW = QW + 2 * HD
    pieces = PIECES
    messages = (N - 1) * pieces // 2
    sharing = N // (key_value_weight.shape[3] // HD)
    cos_table, sin_table = rope_tables(T)
    anywhere = pl.BlockSpec(memory_space=pl.ANY)
    dma = pltpu.SemaphoreType.DMA
    return pl.pallas_call(
        functools.partial(body, N, S, sharing),
        out_shape=(
            jax.ShapeDtypeStruct((1, T, F), BF16),
            jax.ShapeDtypeStruct((1, 1, R, F), F32),
            jax.ShapeDtypeStruct((1, 1, R, F), F32),
        ),
        in_specs=[anywhere] * 8 + [pl.BlockSpec(memory_space=pltpu.SMEM)] + [anywhere] * 2,
        out_specs=(anywhere,) * 3,
        scratch_shapes=[
            pltpu.VMEM((N, T, F), BF16),
            pltpu.VMEM((N, T, F), BF16),
            pltpu.VMEM((N, T, F), BF16),
            pltpu.VMEM((N, T, KW + LANES), BF16),
            pltpu.VMEM((N, T, KW + LANES), BF16),
            pltpu.VMEM((T, QW + LANES), BF16),
            pltpu.VMEM((N, T, QW + LANES), BF16),
            pltpu.VMEM((2, messages, T // pieces, F), BF16),
            pltpu.VMEM((2, messages, T // pieces, F), BF16),
            pltpu.VMEM((2, T, F), F32),
            pltpu.VMEM((F, KW), BF16),
            pltpu.VMEM((QW, F), BF16),
            pltpu.VMEM((LANES, F), BF16),
            pltpu.VMEM((LANES, F), BF16),
            pltpu.VMEM((1, F), F32),
            pltpu.VMEM((1, F), F32),
            pltpu.VMEM((T, HD), F32),
            pltpu.VMEM((T, HD), F32),
            pltpu.VMEM((N, T, LANES), BF16),
            pltpu.VMEM((N, T, LANES), BF16),
            pltpu.VMEM((N, T, LANES), BF16),
            pltpu.VMEM((T, F), BF16),
            pltpu.VMEM((LANES, F), F32),
            pltpu.VMEM((LANES, F), F32),
            dma((10,)),
            dma((1,)),
            dma((1,)),
            dma((1,)),
            dma((pieces,)),
            dma((1,)),
            dma((2, messages)),
            dma((1,)),
            dma((2, messages)),
            dma((1,)),
            dma((1,)),
            dma((1,)),
            dma((N,)),
            dma((1,)),
            dma((2, messages)),
            dma((1,)),
            dma((N,)),
            dma((1,)),
            dma((1,)),
            dma((1,)),
            dma((1,)),
            dma((1,)),
            dma((1,)),
        ],
        compiler_params=pltpu.CompilerParams(
            collective_id=0, has_side_effects=True, vmem_limit_bytes=56 * 1024 * 1024
        ),
    )(
        inputs,
        parent_gain,
        query_weight,
        key_value_weight,
        output_weight,
        candidate_gain,
        candidate_down,
        candidate_up,
        kept_ranks,
        jnp.asarray(cos_table),
        jnp.asarray(sin_table),
    )


def solution(mesh):
    placed = (
        P("dp", "cand"),
        P("section", None),
        P("section", "dp", "cand"),
        P("section", None, "dp", None),
        P("section", "cand", "dp"),
        P("section", "cand", None),
        P("section", "cand", None, None),
        P("section", "cand", None, None),
        P("section", "cand"),
    )
    return jax.shard_map(
        shards,
        mesh=mesh,
        in_specs=placed,
        out_specs=(
            P("section", "dp", "cand"),
            P("section", "cand", None, "dp"),
            P("section", "cand", None, "dp"),
        ),
        check_vma=False,
    )
```

```python
import functools

import jax
import jax.numpy as jnp
import numpy as np
from jax import lax
from jax.experimental import pallas as pl
from jax.experimental.pallas import tpu as pltpu
from jax.sharding import PartitionSpec as P

HD = 128
LANES = 128
PIECES = 4
EPSILON = 1e-05
ROPE_BASE = 500000.0
MESH = pl.DeviceIdType.MESH
F32 = jnp.float32
BF16 = jnp.bfloat16


def dot_nt(a, b):
    return lax.dot_general(a, b, (((1,), (1,)), ((), ())), preferred_element_type=F32)


def dot_tn(a, b):
    return lax.dot_general(a, b, (((0,), (0,)), ((), ())), preferred_element_type=F32)


def rope_tables(tokens):
    half = HD // 2
    frequency = (ROPE_BASE ** (-np.arange(half, dtype=np.float64) / half)).astype(np.float32)
    angles = np.arange(tokens, dtype=np.float32)[:, None] * frequency[None, :]
    angles = angles.astype(np.float64)
    cosine, sine = np.cos(angles), np.sin(angles)
    full_cos = np.concatenate([cosine, cosine], axis=1).astype(np.float32)
    full_sin = np.concatenate([-sine, sine], axis=1).astype(np.float32)
    return full_cos, full_sin


def body(
    N,
    S,
    sharing,
    inputs,
    parent_gain,
    query_weight,
    key_value_weight,
    output_weight,
    candidate_gain,
    candidate_down,
    candidate_up,
    kept,
    cos_table,
    sin_table,
    states_out,
    down_out,
    up_out,
    x_buf,
    st_buf,
    sc_buf,
    p_buf,
    r_buf,
    a_own,
    a_buf,
    s_send,
    s_recv,
    part,
    w_qkv,
    w_out,
    w_down,
    w_up,
    pg,
    cg,
    cos_v,
    sin_v,
    bw_send,
    bw_recv,
    bw_all,
    last_send,
    last_recv,
    y_mid,
    y_buf,
    g_down,
    g_up,
    load_sem,
    in_send,
    in_recv,
    nx_send,
    nx_recv,
    ag_send,
    ag_recv,
    sg_send,
    sg_recv,
    p_send,
    p_recv,
    a_send,
    a_recv,
    rs_send,
    rs_recv,
    mate_send,
    mate_recv,
    y_send,
    y_recv,
    b_send,
    b_recv,
    c_send,
    c_recv,
    d_send,
    d_recv,
    m_send,
    m_recv,
):
    s = lax.axis_index("section")
    z = lax.axis_index("cand")
    i = lax.axis_index("dp")
    T, F = inputs.shape
    R = candidate_down.shape[2]
    D = N * F
    QW = query_weight.shape[2]
    heads = QW // HD
    KW = QW + 2 * HD
    piece = T // N
    token_total = T * N
    middle = N // 2

    def wrap(index):
        return lax.rem(index + 2 * N, N)

    def rows(index):
        return pl.ds(pl.multiple_of(index * piece, piece), piece)

    def remote(source, target, send, recv, **device):
        return pltpu.make_async_remote_copy(
            src_ref=source,
            dst_ref=target,
            send_sem=send,
            recv_sem=recv,
            device_id=device,
            device_id_type=MESH,
        )

    def wait_bytes(ref, sem):
        pltpu.make_async_copy(ref, ref, sem).wait()

    features = pl.ds(pl.multiple_of(i * F, F), F)
    kv_columns = pl.ds(pl.multiple_of((z // sharing) * HD, HD), HD)
    loads = [
        (query_weight.at[0], w_qkv.at[:, pl.ds(0, QW)]),
        (key_value_weight.at[0, 0, :, kv_columns], w_qkv.at[:, pl.ds(QW, HD)]),
        (key_value_weight.at[0, 1, :, kv_columns], w_qkv.at[:, pl.ds(QW + HD, HD)]),
        (output_weight.at[0], w_out),
        (candidate_down.at[0, 0, :, features], w_down.at[pl.ds(0, R)]),
        (candidate_up.at[0, 0, :, features], w_up.at[pl.ds(0, R)]),
        (parent_gain.at[:, features], pg),
        (candidate_gain.at[0, :, features], cg),
        (cos_table, cos_v),
        (sin_table, sin_v),
    ]
    copies = [
        pltpu.make_async_copy(source, target, load_sem.at[k])
        for k, (source, target) in enumerate(loads)
    ]
    for copy in copies:
        copy.start()

    barrier = pltpu.get_barrier_semaphore()

    def greet(**device):
        pl.semaphore_signal(barrier, inc=1, device_id=device, device_id_type=MESH)

    diagonal = i == z
    odd = lax.rem(s, 2) == 1
    for k in range(1, N):
        greet(cand=wrap(z + k))
        greet(dp=wrap(i + k))
    for w in range(N):

        @pl.when(jnp.logical_not(diagonal & (z == w)))
        def _(w=w):
            greet(dp=z, cand=w)
            greet(dp=w, cand=i)

    @pl.when(s > 0)
    def _():
        greet(section=s - 1)

    @pl.when(s < S - 1)
    def _():
        greet(section=s + 1)

    mate = s + 1 - 2 * lax.rem(s, 2)
    greet(section=mate, cand=wrap(z + 1))
    greet(section=mate, cand=wrap(z - 1))

    expected = (
        2
        + 2 * (N - 1)
        + 2 * N
        - 2 * diagonal.astype(jnp.int32)
        + (s > 0).astype(jnp.int32)
        + (s < S - 1).astype(jnp.int32)
    )
    pl.semaphore_wait(barrier, expected)

    pieces = PIECES
    messages = (N - 1) * pieces // 2
    piece_rows = T // pieces

    def part_rows(q):
        return pl.ds(q * piece_rows, piece_rows)

    def piece_of(way, k):
        return k % pieces if way == 0 else pieces - 1 - k % pieces

    def toward(way):
        return wrap(z + 1 - 2 * way)

    def send_input():
        for w in range(N):
            source = inputs.at[pl.ds(w * piece, piece)]
            target = x_buf.at[w, rows(i)]
            own = diagonal & (z == w)

            @pl.when(own)
            def _(source=source, target=target):
                pltpu.make_async_copy(source, target, in_recv.at[0]).start()

            @pl.when(jnp.logical_not(own))
            def _(source=source, target=target, w=w):
                remote(source, target, in_send.at[0], in_recv.at[0], dp=z, cand=w).start()

    def wait_pieces_sent(sem):
        @pl.when(diagonal)
        def _():
            wait_bytes(y_buf.at[pl.ds(0, T - piece)], sem)

        @pl.when(jnp.logical_not(diagonal))
        def _():
            wait_bytes(y_buf, sem)

    def prepare():
        for copy in copies:
            copy.wait()
        w_down[pl.ds(R, LANES - R), :] = jnp.zeros((LANES - R, F), BF16)
        w_up[pl.ds(R, LANES - R), :] = jnp.zeros((LANES - R, F), BF16)
        w_down[pl.ds(0, R), :] = (w_down[pl.ds(0, R), :].astype(F32) * cg[...]).astype(BF16)

    def relay(source, target, block, distance, way, k, send, recv, **device):
        place = part_rows(piece_of(way, k))
        if distance < middle - 1 or (distance == middle - 1 and k < pieces // 2):
            remote(
                source.at[block, place],
                target.at[block, place],
                send.at[0],
                recv.at[way, distance * pieces + k],
                cand=toward(way),
                **device,
            ).start()

    def gather_step(buffer, k, send, recv):
        distance = k // pieces + 1
        for way in (0, 1):
            block = wrap(z - distance + 2 * distance * way)
            wait_bytes(buffer.at[block, part_rows(piece_of(way, k))], recv.at[way, k])
            relay(buffer, buffer, block, distance, way, k % pieces, send, recv)

    start_order = []
    for q in range(pieces // 2):
        start_order += [q, pieces - 1 - q]
    ready = []
    for n in range(pieces):
        done = set(start_order[: n + 1])
        fresh = []
        for way in (0, 1):
            for k in range(pieces):
                before = all(piece_of(way, b) in done for b in range(k + 1))
                if before and not any((way, k) in earlier for earlier in ready):
                    fresh.append((way, k))
        ready.append(fresh)

    def relay_ready(source, target, n, send, recv, **device):
        for way, k in ready[n]:
            relay(source, target, z, 0, way, k, send, recv, **device)

    lane = lax.broadcasted_iota(jnp.int32, (T, LANES), 1)
    keep = (lax.broadcasted_iota(jnp.int32, (1, LANES), 1) < kept[0, 0]).astype(F32)

    def project(block):
        values = x_buf[block]
        wide = values.astype(F32)
        scaled = (wide * pg[...]).astype(BF16)
        p_buf[block, :, pl.ds(0, KW)] = jnp.dot(
            scaled, w_qkv[...], preferred_element_type=F32
        ).astype(BF16)
        hidden = dot_nt(values, w_down[...])
        squares = jnp.sum(wide * wide, axis=-1, keepdims=True)
        coarse = squares.astype(BF16).astype(F32)
        extra = jnp.where(lane == R, coarse, jnp.where(lane == R + 1, squares - coarse, hidden))
        p_buf[block, :, pl.ds(KW, LANES)] = extra.astype(BF16)
        for k in range(1, N):
            t = wrap(i + k)
            remote(
                p_buf.at[block, rows(t)],
                r_buf.at[i, rows(block)],
                p_send.at[0],
                p_recv.at[0],
                dp=t,
            ).start()
        r_buf[i, rows(block), :] = p_buf[block, rows(i), :]

    def mate_copy(d):
        place = wrap(z + d)
        remote(
            x_buf.at[place], st_buf.at[place], mate_send.at[0], mate_recv.at[d], section=s - 1
        ).start()

    def gather_and_project():
        @pl.when(s == 0)
        def _():
            wait_bytes(x_buf.at[z], in_recv.at[0])

        for n, q in enumerate(start_order):

            @pl.when(s > 0)
            def _(q=q):
                wait_bytes(x_buf.at[z, part_rows(q)], nx_recv.at[q])

            @pl.when(jnp.logical_not(odd))
            def _(n=n):
                relay_ready(x_buf, x_buf, n, ag_send, ag_recv)

        project(z)
        for j in range(middle):
            for k in range(j * pieces, min((j + 1) * pieces, messages)):
                gather_step(x_buf, k, ag_send, ag_recv)
            project(wrap(z + j + 1))
            if j < middle - 1:
                project(wrap(z - j - 1))

                @pl.when(odd)
                def _(j=j):
                    mate_copy(j + 1)
                    mate_copy(N - j - 1)


    def summed(b):
        total = r_buf[0, :, pl.ds(b * LANES, LANES)].astype(F32)
        for source in range(1, N):
            total += r_buf[source, :, pl.ds(b * LANES, LANES)].astype(F32)
        return total

    def rotated(matrix):
        return (matrix * cos_v[...] + pltpu.roll(matrix, HD // 2, 1) * sin_v[...]).astype(BF16)

    offsets = [middle]
    for m in range(middle - 1, 0, -1):
        offsets += [m, -m]
    offsets.append(0)

    def attention():
        wait_bytes(r_buf.at[pl.ds(0, N - 1)], p_recv.at[0])
        extra = summed(heads + 2)
        squares = extra[:, R : R + 1] + extra[:, R + 1 : R + 2]
        inverse = lax.rsqrt(squares / D + EPSILON)
        hidden = extra * inverse * keep
        inverse_coarse = inverse.astype(BF16).astype(F32)
        a_own[:, pl.ds(QW, LANES)] = jnp.where(
            lane == R, inverse_coarse, jnp.where(lane == R + 1, inverse - inverse_coarse, hidden)
        ).astype(BF16)
        keys = rotated(summed(heads) * inverse)
        values = (summed(heads + 1) * inverse).astype(BF16)
        allowed = lax.broadcasted_iota(jnp.int32, (T, T), 1) <= lax.broadcasted_iota(
            jnp.int32, (T, T), 0
        )
        for h in range(heads):
            queries = rotated(summed(h) * inverse)
            scores = dot_nt(queries, keys) * HD ** (-0.5)
            raised = jnp.where(allowed, jnp.exp(scores), 0.0)
            weights = (raised / jnp.sum(raised, axis=-1, keepdims=True)).astype(BF16)
            a_own[:, pl.ds(h * HD, HD)] = jnp.dot(
                weights, values, preferred_element_type=F32
            ).astype(BF16)
        for d, offset in enumerate(offsets):
            block = wrap(z + offset)
            for k in range(1, N):
                remote(
                    a_own.at[rows(block)],
                    a_buf.at[block, rows(i)],
                    a_send.at[0],
                    a_recv.at[d],
                    dp=wrap(i + k),
                ).start()
            a_buf[block, rows(i), :] = a_own[rows(block), :]

    def project_out(slot, offset):
        block = wrap(z + offset)
        wait_bytes(a_buf.at[block, pl.ds(0, T - piece)], a_recv.at[offsets.index(offset)])
        part[slot] = jnp.dot(
            a_buf[block, :, pl.ds(0, QW)], w_out[...], preferred_element_type=F32
        )

    def got(way, k):
        wait_bytes(s_recv.at[way, k], rs_recv.at[way, k])
        return s_recv[way, k].astype(F32)

    def slot_of(offset, k):
        return pieces // 2 + (middle - 1 - offset) * pieces + k

    def contribution(offset, way, k):
        if offset < middle - 1:
            return got(way, slot_of(offset + 1, k))
        return got(way, k) if k < pieces // 2 else 0.0

    def emit(way, slot, value):
        s_send[way, slot] = value.astype(BF16)
        remote(
            s_send.at[way, slot],
            s_recv.at[way, slot],
            rs_send.at[0],
            rs_recv.at[way, slot],
            cand=toward(way),
        ).start()

    arrival_order = list(range(pieces // 2, pieces)) + list(range(pieces // 2))

    def next_piece(q):
        remote(
            st_buf.at[z, part_rows(q)],
            x_buf.at[z, part_rows(q)],
            nx_send.at[0],
            nx_recv.at[q],
            section=s + 1,
        ).start()

    def hand_on(n):
        @pl.when(jnp.logical_not(odd))
        def _():
            relay_ready(st_buf, x_buf, n, nx_send, ag_recv, section=s + 1)

        @pl.when(odd & (s < S - 1))
        def _():
            next_piece(start_order[n])

        @pl.when(s == S - 1)
        def _():
            relay_ready(st_buf, st_buf, n, sg_send, sg_recv)

    def output():
        project_out(0, middle)
        for k in range(pieces // 2):
            for way in (0, 1):
                emit(way, k, part[0, part_rows(piece_of(way, k)), :])
        for m in range(middle - 1, 0, -1):
            project_out(0, m)
            project_out(1, -m)
            for k in arrival_order:
                for way in (0, 1):
                    value = part[way, part_rows(piece_of(way, k)), :]
                    emit(way, slot_of(m, k), value + contribution(m, way, k))
        project_out(0, 0)
        for n, q in enumerate(start_order):
            place = part_rows(q)
            total = x_buf[z, place, :].astype(F32) + part[0, place, :]
            for way in (0, 1):
                total += contribution(0, way, piece_of(way, q))
            st_buf[z, place, :] = total.astype(BF16)
            hand_on(n)

    def hand_over():
        @pl.when(odd)
        def _():
            @pl.when(s < S - 1)
            def _():
                wait_bytes(x_buf.at[0], nx_send.at[0])
                for n in range(pieces):
                    relay_ready(st_buf, st_buf, n, sg_send, sg_recv)

            mate_copy(middle)

        send_state()

        @pl.when(jnp.logical_not(odd))
        def _():
            for q in range(pieces):
                next_piece(q)

    def send_state():
        for k in range(1, N):
            t = wrap(i + k)
            remote(
                st_buf.at[z, rows(t)], y_mid.at[i], m_send.at[0], m_recv.at[0], dp=t
            ).start()
        y_mid[i] = st_buf[z, rows(i), :]

    def pass_state():
        wait_bytes(y_mid.at[pl.ds(0, N - 1)], m_recv.at[0])
        for k in range(1, N):
            w = wrap(z + k)
            remote(
                y_mid.at[w], y_buf.at[rows(z)], y_send.at[0], y_recv.at[0], cand=w
            ).start()
        y_buf[rows(z), :] = y_mid[z]

    farthest = wrap(z + middle)

    def candidate(block, last=False):
        hidden = a_buf[block, :, pl.ds(QW, LANES)]
        branch = jnp.dot(hidden, w_up[...], preferred_element_type=F32)
        difference = branch - (st_buf[block].astype(F32) - x_buf[block].astype(F32))
        scaled = (difference * (1.0 / token_total)).astype(BF16)
        sc_buf[block] = scaled
        backward = dot_nt(scaled, w_up[...]).astype(BF16)
        if last:
            last_send[...] = backward
            for k in range(1, N):
                remote(
                    last_send, last_recv.at[i], d_send.at[0], d_recv.at[0], dp=wrap(i + k)
                ).start()
            last_recv[i] = backward
            return
        bw_send[block] = backward

        @pl.when(block == i)
        def _():
            bw_recv[i] = bw_send[block]

        @pl.when(block != i)
        def _():
            remote(
                bw_send.at[block], bw_recv.at[i], b_send.at[0], b_recv.at[0], dp=block
            ).start()

    def candidates():
        @pl.when(jnp.logical_not(odd))
        def _():
            wait_bytes(st_buf.at[wrap(z + middle)], mate_recv.at[middle])

        candidate(z)
        for j in range(middle):
            last = j == middle - 1

            @pl.when(odd)
            def _(j=j):
                for k in range(j * pieces, min((j + 1) * pieces, messages)):
                    gather_step(st_buf, k, sg_send, sg_recv)

            @pl.when(jnp.logical_not(odd))
            def _(j=j, last=last):
                if not last:
                    wait_bytes(st_buf.at[wrap(z + j + 1)], mate_recv.at[j + 1])
                    wait_bytes(st_buf.at[wrap(z - j - 1)], mate_recv.at[N - j - 1])

            candidate(wrap(z + j + 1), last)
            if not last:
                candidate(wrap(z - j - 1))


    def gradients():
        def finish(block, received):
            backward = received[0].astype(F32)
            for source in range(1, N):
                backward += received[source].astype(F32)
            extra = a_buf[block, :, pl.ds(QW, LANES)].astype(F32)
            inverse = extra[:, R : R + 1] + extra[:, R + 1 : R + 2]
            bw_all[block] = (backward * keep * inverse).astype(BF16)

        @pl.when(i != farthest)
        def _():
            wait_bytes(bw_recv.at[pl.ds(0, N - 1)], b_recv.at[0])
            finish(i, bw_recv)
            for k in range(1, N):
                remote(
                    bw_all.at[i], bw_all.at[i], c_send.at[0], c_recv.at[0], dp=wrap(i + k)
                ).start()

        hidden_all = a_buf[:, :, pl.ds(QW, LANES)].reshape(N * T, LANES)
        g_up[...] = dot_tn(hidden_all, sc_buf[...].reshape(N * T, F))
        up_copy = pltpu.make_async_copy(g_up.at[pl.ds(0, R)], up_out.at[0, 0], load_sem.at[0])
        up_copy.start()
        pass_state()

        wait_bytes(last_recv.at[pl.ds(0, N - 1)], d_recv.at[0])
        finish(farthest, last_recv)

        @pl.when(i != farthest)
        def _():
            wait_bytes(bw_all.at[pl.ds(0, N - 2)], c_recv.at[0])

        @pl.when(i == farthest)
        def _():
            wait_bytes(bw_all.at[pl.ds(0, N - 1)], c_recv.at[0])

        g_down[...] = (
            dot_tn(bw_all[...].reshape(N * T, LANES), x_buf[...].reshape(N * T, F)) * cg[...]
        )
        down_copy = pltpu.make_async_copy(
            g_down.at[pl.ds(0, R)], down_out.at[0, 0], load_sem.at[2]
        )
        down_copy.start()
        wait_bytes(y_buf.at[pl.ds(0, T - piece)], y_recv.at[0])
        y_copy = pltpu.make_async_copy(y_buf, states_out.at[0], load_sem.at[1])
        y_copy.start()
        up_copy.wait()
        y_copy.wait()
        down_copy.wait()

    def drain():
        @pl.when(s == 0)
        def _():
            wait_pieces_sent(in_send.at[0])

        others = pl.ds(0, N - 1)

        @pl.when(jnp.logical_not(odd))
        def _():
            wait_bytes(x_buf.at[others], ag_send.at[0])
            wait_bytes(x_buf.at[pl.ds(0, 3)], nx_send.at[0])

        @pl.when(odd)
        def _():
            wait_bytes(x_buf.at[pl.ds(0, N - 3)], ag_send.at[0])
            wait_bytes(st_buf.at[others], sg_send.at[0])
            wait_bytes(st_buf.at[others], mate_send.at[0])

        wait_bytes(p_buf.at[others], p_send.at[0])
        wait_bytes(a_buf.at[others], a_send.at[0])
        wait_bytes(s_send, rs_send.at[0])
        wait_bytes(y_mid.at[others], m_send.at[0])
        wait_bytes(y_mid.at[others], y_send.at[0])
        wait_bytes(last_recv.at[others], d_send.at[0])

        @pl.when(i != farthest)
        def _():
            wait_bytes(bw_send.at[pl.ds(0, N - 2)], b_send.at[0])
            wait_bytes(bw_all.at[others], c_send.at[0])

        @pl.when(i == farthest)
        def _():
            wait_bytes(bw_send.at[others], b_send.at[0])

    @pl.when(s == 0)
    def _():
        send_input()

    prepare()
    gather_and_project()
    attention()
    output()
    hand_over()
    candidates()
    gradients()
    drain()


def shards(
    inputs,
    parent_gain,
    query_weight,
    key_value_weight,
    output_weight,
    candidate_gain,
    candidate_down,
    candidate_up,
    kept_ranks,
):
    N = lax.axis_size("cand")
    S = lax.axis_size("section")
    T, F = inputs.shape
    R = candidate_down.shape[2]
    QW = query_weight.shape[2]
    KW = QW + 2 * HD
    pieces = PIECES
    messages = (N - 1) * pieces // 2
    sharing = N // (key_value_weight.shape[3] // HD)
    cos_table, sin_table = rope_tables(T)
    anywhere = pl.BlockSpec(memory_space=pl.ANY)
    dma = pltpu.SemaphoreType.DMA
    return pl.pallas_call(
        functools.partial(body, N, S, sharing),
        out_shape=(
            jax.ShapeDtypeStruct((1, T, F), BF16),
            jax.ShapeDtypeStruct((1, 1, R, F), F32),
            jax.ShapeDtypeStruct((1, 1, R, F), F32),
        ),
        in_specs=[anywhere] * 8 + [pl.BlockSpec(memory_space=pltpu.SMEM)] + [anywhere] * 2,
        out_specs=(anywhere,) * 3,
        scratch_shapes=[
            pltpu.VMEM((N, T, F), BF16),
            pltpu.VMEM((N, T, F), BF16),
            pltpu.VMEM((N, T, F), BF16),
            pltpu.VMEM((N, T, KW + LANES), BF16),
            pltpu.VMEM((N, T, KW + LANES), BF16),
            pltpu.VMEM((T, QW + LANES), BF16),
            pltpu.VMEM((N, T, QW + LANES), BF16),
            pltpu.VMEM((2, messages, T // pieces, F), BF16),
            pltpu.VMEM((2, messages, T // pieces, F), BF16),
            pltpu.VMEM((2, T, F), F32),
            pltpu.VMEM((F, KW), BF16),
            pltpu.VMEM((QW, F), BF16),
            pltpu.VMEM((LANES, F), BF16),
            pltpu.VMEM((LANES, F), BF16),
            pltpu.VMEM((1, F), F32),
            pltpu.VMEM((1, F), F32),
            pltpu.VMEM((T, HD), F32),
            pltpu.VMEM((T, HD), F32),
            pltpu.VMEM((N, T, LANES), BF16),
            pltpu.VMEM((N, T, LANES), BF16),
            pltpu.VMEM((N, T, LANES), BF16),
            pltpu.VMEM((T, LANES), BF16),
            pltpu.VMEM((N, T, LANES), BF16),
            pltpu.VMEM((N, T // N, F), BF16),
            pltpu.VMEM((T, F), BF16),
            pltpu.VMEM((LANES, F), F32),
            pltpu.VMEM((LANES, F), F32),
            dma((10,)),
            dma((1,)),
            dma((1,)),
            dma((1,)),
            dma((pieces,)),
            dma((1,)),
            dma((2, messages)),
            dma((1,)),
            dma((2, messages)),
            dma((1,)),
            dma((1,)),
            dma((1,)),
            dma((N,)),
            dma((1,)),
            dma((2, messages)),
            dma((1,)),
            dma((N,)),
            dma((1,)),
            dma((1,)),
            dma((1,)),
            dma((1,)),
            dma((1,)),
            dma((1,)),
            dma((1,)),
            dma((1,)),
            dma((1,)),
            dma((1,)),
        ],
        compiler_params=pltpu.CompilerParams(
            collective_id=0, has_side_effects=True, vmem_limit_bytes=56 * 1024 * 1024
        ),
    )(
        inputs,
        parent_gain,
        query_weight,
        key_value_weight,
        output_weight,
        candidate_gain,
        candidate_down,
        candidate_up,
        kept_ranks,
        jnp.asarray(cos_table),
        jnp.asarray(sin_table),
    )


def solution(mesh):
    placed = (
        P("dp", "cand"),
        P("section", None),
        P("section", "dp", "cand"),
        P("section", None, "dp", None),
        P("section", "cand", "dp"),
        P("section", "cand", None),
        P("section", "cand", None, None),
        P("section", "cand", None, None),
        P("section", "cand"),
    )
    return jax.shard_map(
        shards,
        mesh=mesh,
        in_specs=placed,
        out_specs=(
            P("section", "dp", "cand"),
            P("section", "cand", None, "dp"),
            P("section", "cand", None, "dp"),
        ),
        check_vma=False,
    )
```

```python
import functools

import jax
import jax.numpy as jnp
import numpy as np
from jax import lax
from jax.experimental import pallas as pl
from jax.experimental.pallas import tpu as pltpu
from jax.sharding import PartitionSpec as P

HD = 128
LANES = 128
PIECES = 8
EPSILON = 1e-05
ROPE_BASE = 500000.0
MESH = pl.DeviceIdType.MESH
F32 = jnp.float32
BF16 = jnp.bfloat16


def dot_nt(a, b):
    return lax.dot_general(a, b, (((1,), (1,)), ((), ())), preferred_element_type=F32)


def dot_tn(a, b):
    return lax.dot_general(a, b, (((0,), (0,)), ((), ())), preferred_element_type=F32)


def rope_tables(tokens):
    half = HD // 2
    frequency = (ROPE_BASE ** (-np.arange(half, dtype=np.float64) / half)).astype(np.float32)
    angles = np.arange(tokens, dtype=np.float32)[:, None] * frequency[None, :]
    angles = angles.astype(np.float64)
    cosine, sine = np.cos(angles), np.sin(angles)
    full_cos = np.concatenate([cosine, cosine], axis=1).astype(np.float32)
    full_sin = np.concatenate([-sine, sine], axis=1).astype(np.float32)
    return full_cos, full_sin


def body(
    N,
    S,
    sharing,
    inputs,
    parent_gain,
    query_weight,
    key_value_weight,
    output_weight,
    candidate_gain,
    candidate_down,
    candidate_up,
    kept,
    cos_table,
    sin_table,
    states_out,
    down_out,
    up_out,
    x_buf,
    st_buf,
    sc_buf,
    p_buf,
    r_buf,
    a_own,
    a_buf,
    s_send,
    s_recv,
    part,
    w_qkv,
    w_out,
    w_down,
    w_up,
    pg,
    cg,
    cos_v,
    sin_v,
    bw_send,
    bw_recv,
    bw_all,
    last_send,
    last_recv,
    y_mid,
    y_buf,
    g_down,
    g_up,
    load_sem,
    in_send,
    in_recv,
    nx_send,
    nx_recv,
    ag_send,
    ag_recv,
    sg_send,
    sg_recv,
    p_send,
    p_recv,
    a_send,
    a_recv,
    rs_send,
    rs_recv,
    mate_send,
    mate_recv,
    y_send,
    y_recv,
    b_send,
    b_recv,
    c_send,
    c_recv,
    d_send,
    d_recv,
    m_send,
    m_recv,
):
    s = lax.axis_index("section")
    z = lax.axis_index("cand")
    i = lax.axis_index("dp")
    T, F = inputs.shape
    R = candidate_down.shape[2]
    D = N * F
    QW = query_weight.shape[2]
    heads = QW // HD
    KW = QW + 2 * HD
    piece = T // N
    token_total = T * N
    middle = N // 2

    def wrap(index):
        return lax.rem(index + 2 * N, N)

    def rows(index):
        return pl.ds(pl.multiple_of(index * piece, piece), piece)

    def remote(source, target, send, recv, **device):
        return pltpu.make_async_remote_copy(
            src_ref=source,
            dst_ref=target,
            send_sem=send,
            recv_sem=recv,
            device_id=device,
            device_id_type=MESH,
        )

    def wait_bytes(ref, sem):
        pltpu.make_async_copy(ref, ref, sem).wait()

    features = pl.ds(pl.multiple_of(i * F, F), F)
    kv_columns = pl.ds(pl.multiple_of((z // sharing) * HD, HD), HD)
    loads = [
        (query_weight.at[0], w_qkv.at[:, pl.ds(0, QW)]),
        (key_value_weight.at[0, 0, :, kv_columns], w_qkv.at[:, pl.ds(QW, HD)]),
        (key_value_weight.at[0, 1, :, kv_columns], w_qkv.at[:, pl.ds(QW + HD, HD)]),
        (output_weight.at[0], w_out),
        (candidate_down.at[0, 0, :, features], w_down.at[pl.ds(0, R)]),
        (candidate_up.at[0, 0, :, features], w_up.at[pl.ds(0, R)]),
        (parent_gain.at[:, features], pg),
        (candidate_gain.at[0, :, features], cg),
        (cos_table, cos_v),
        (sin_table, sin_v),
    ]
    copies = [
        pltpu.make_async_copy(source, target, load_sem.at[k])
        for k, (source, target) in enumerate(loads)
    ]
    for copy in copies:
        copy.start()

    barrier = pltpu.get_barrier_semaphore()

    def greet(**device):
        pl.semaphore_signal(barrier, inc=1, device_id=device, device_id_type=MESH)

    diagonal = i == z
    odd = lax.rem(s, 2) == 1
    for k in range(1, N):
        greet(cand=wrap(z + k))
        greet(dp=wrap(i + k))
    for w in range(N):

        @pl.when(jnp.logical_not(diagonal & (z == w)))
        def _(w=w):
            greet(dp=z, cand=w)
            greet(dp=w, cand=i)

    @pl.when(s > 0)
    def _():
        greet(section=s - 1)

    @pl.when(s < S - 1)
    def _():
        greet(section=s + 1)

    mate = s + 1 - 2 * lax.rem(s, 2)
    greet(section=mate, cand=wrap(z + 1))
    greet(section=mate, cand=wrap(z - 1))

    expected = (
        2
        + 2 * (N - 1)
        + 2 * N
        - 2 * diagonal.astype(jnp.int32)
        + (s > 0).astype(jnp.int32)
        + (s < S - 1).astype(jnp.int32)
    )
    pl.semaphore_wait(barrier, expected)

    pieces = PIECES
    messages = (N - 1) * pieces // 2
    piece_rows = T // pieces

    def part_rows(q):
        return pl.ds(q * piece_rows, piece_rows)

    def piece_of(way, k):
        return k % pieces if way == 0 else pieces - 1 - k % pieces

    def toward(way):
        return wrap(z + 1 - 2 * way)

    def send_input():
        for w in range(N):
            source = inputs.at[pl.ds(w * piece, piece)]
            target = x_buf.at[w, rows(i)]
            own = diagonal & (z == w)

            @pl.when(own)
            def _(source=source, target=target):
                pltpu.make_async_copy(source, target, in_recv.at[0]).start()

            @pl.when(jnp.logical_not(own))
            def _(source=source, target=target, w=w):
                remote(source, target, in_send.at[0], in_recv.at[0], dp=z, cand=w).start()

    def wait_pieces_sent(sem):
        @pl.when(diagonal)
        def _():
            wait_bytes(y_buf.at[pl.ds(0, T - piece)], sem)

        @pl.when(jnp.logical_not(diagonal))
        def _():
            wait_bytes(y_buf, sem)

    def prepare():
        for copy in copies:
            copy.wait()
        w_down[pl.ds(R, LANES - R), :] = jnp.zeros((LANES - R, F), BF16)
        w_up[pl.ds(R, LANES - R), :] = jnp.zeros((LANES - R, F), BF16)
        w_down[pl.ds(0, R), :] = (w_down[pl.ds(0, R), :].astype(F32) * cg[...]).astype(BF16)

    def relay(source, target, block, distance, way, k, send, recv, **device):
        place = part_rows(piece_of(way, k))
        if distance < middle - 1 or (distance == middle - 1 and k < pieces // 2):
            remote(
                source.at[block, place],
                target.at[block, place],
                send.at[0],
                recv.at[way, distance * pieces + k],
                cand=toward(way),
                **device,
            ).start()

    def gather_step(buffer, k, send, recv):
        distance = k // pieces + 1
        for way in (0, 1):
            block = wrap(z - distance + 2 * distance * way)
            wait_bytes(buffer.at[block, part_rows(piece_of(way, k))], recv.at[way, k])
            relay(buffer, buffer, block, distance, way, k % pieces, send, recv)

    start_order = []
    for q in range(pieces // 2):
        start_order += [q, pieces - 1 - q]
    ready = []
    for n in range(pieces):
        done = set(start_order[: n + 1])
        fresh = []
        for way in (0, 1):
            for k in range(pieces):
                before = all(piece_of(way, b) in done for b in range(k + 1))
                if before and not any((way, k) in earlier for earlier in ready):
                    fresh.append((way, k))
        ready.append(fresh)

    def relay_ready(source, target, n, send, recv, **device):
        for way, k in ready[n]:
            relay(source, target, z, 0, way, k, send, recv, **device)

    lane = lax.broadcasted_iota(jnp.int32, (T, LANES), 1)
    keep = (lax.broadcasted_iota(jnp.int32, (1, LANES), 1) < kept[0, 0]).astype(F32)

    def project(block):
        values = x_buf[block]
        wide = values.astype(F32)
        scaled = (wide * pg[...]).astype(BF16)
        p_buf[block, :, pl.ds(0, KW)] = jnp.dot(
            scaled, w_qkv[...], preferred_element_type=F32
        ).astype(BF16)
        hidden = dot_nt(values, w_down[...])
        squares = jnp.sum(wide * wide, axis=-1, keepdims=True)
        coarse = squares.astype(BF16).astype(F32)
        extra = jnp.where(lane == R, coarse, jnp.where(lane == R + 1, squares - coarse, hidden))
        p_buf[block, :, pl.ds(KW, LANES)] = extra.astype(BF16)
        for k in range(1, N):
            t = wrap(i + k)
            remote(
                p_buf.at[block, rows(t)],
                r_buf.at[i, rows(block)],
                p_send.at[0],
                p_recv.at[0],
                dp=t,
            ).start()
        r_buf[i, rows(block), :] = p_buf[block, rows(i), :]

    def mate_copy(d):
        place = wrap(z + d)
        remote(
            x_buf.at[place], st_buf.at[place], mate_send.at[0], mate_recv.at[d], section=s - 1
        ).start()

    def gather_and_project():
        @pl.when(s == 0)
        def _():
            wait_bytes(x_buf.at[z], in_recv.at[0])

        for n, q in enumerate(start_order):

            @pl.when(s > 0)
            def _(q=q):
                wait_bytes(x_buf.at[z, part_rows(q)], nx_recv.at[q])

            @pl.when(jnp.logical_not(odd))
            def _(n=n):
                relay_ready(x_buf, x_buf, n, ag_send, ag_recv)

        project(z)
        for j in range(middle):
            for k in range(j * pieces, min((j + 1) * pieces, messages)):
                gather_step(x_buf, k, ag_send, ag_recv)
            project(wrap(z + j + 1))
            if j < middle - 1:
                project(wrap(z - j - 1))

                @pl.when(odd)
                def _(j=j):
                    mate_copy(j + 1)
                    mate_copy(N - j - 1)


    def summed(b):
        total = r_buf[0, :, pl.ds(b * LANES, LANES)].astype(F32)
        for source in range(1, N):
            total += r_buf[source, :, pl.ds(b * LANES, LANES)].astype(F32)
        return total

    def rotated(matrix):
        return (matrix * cos_v[...] + pltpu.roll(matrix, HD // 2, 1) * sin_v[...]).astype(BF16)

    offsets = [middle]
    for m in range(middle - 1, 0, -1):
        offsets += [m, -m]
    offsets.append(0)

    def attention():
        wait_bytes(r_buf.at[pl.ds(0, N - 1)], p_recv.at[0])
        extra = summed(heads + 2)
        squares = extra[:, R : R + 1] + extra[:, R + 1 : R + 2]
        inverse = lax.rsqrt(squares / D + EPSILON)
        hidden = extra * inverse * keep
        inverse_coarse = inverse.astype(BF16).astype(F32)
        a_own[:, pl.ds(QW, LANES)] = jnp.where(
            lane == R, inverse_coarse, jnp.where(lane == R + 1, inverse - inverse_coarse, hidden)
        ).astype(BF16)
        keys = rotated(summed(heads) * inverse)
        values = (summed(heads + 1) * inverse).astype(BF16)
        allowed = lax.broadcasted_iota(jnp.int32, (T, T), 1) <= lax.broadcasted_iota(
            jnp.int32, (T, T), 0
        )
        for h in range(heads):
            queries = rotated(summed(h) * inverse)
            scores = dot_nt(queries, keys) * HD ** (-0.5)
            raised = jnp.where(allowed, jnp.exp(scores), 0.0)
            weights = (raised / jnp.sum(raised, axis=-1, keepdims=True)).astype(BF16)
            a_own[:, pl.ds(h * HD, HD)] = jnp.dot(
                weights, values, preferred_element_type=F32
            ).astype(BF16)
        for d, offset in enumerate(offsets):
            block = wrap(z + offset)
            for k in range(1, N):
                remote(
                    a_own.at[rows(block)],
                    a_buf.at[block, rows(i)],
                    a_send.at[0],
                    a_recv.at[d],
                    dp=wrap(i + k),
                ).start()
            a_buf[block, rows(i), :] = a_own[rows(block), :]

    def project_out(slot, offset):
        block = wrap(z + offset)
        wait_bytes(a_buf.at[block, pl.ds(0, T - piece)], a_recv.at[offsets.index(offset)])
        part[slot] = jnp.dot(
            a_buf[block, :, pl.ds(0, QW)], w_out[...], preferred_element_type=F32
        )

    def got(way, k):
        wait_bytes(s_recv.at[way, k], rs_recv.at[way, k])
        return s_recv[way, k].astype(F32)

    def slot_of(offset, k):
        return pieces // 2 + (middle - 1 - offset) * pieces + k

    def contribution(offset, way, k):
        if offset < middle - 1:
            return got(way, slot_of(offset + 1, k))
        return got(way, k) if k < pieces // 2 else 0.0

    def emit(way, slot, value):
        s_send[way, slot] = value.astype(BF16)
        remote(
            s_send.at[way, slot],
            s_recv.at[way, slot],
            rs_send.at[0],
            rs_recv.at[way, slot],
            cand=toward(way),
        ).start()

    arrival_order = list(range(pieces // 2, pieces)) + list(range(pieces // 2))

    def next_piece(q):
        remote(
            st_buf.at[z, part_rows(q)],
            x_buf.at[z, part_rows(q)],
            nx_send.at[0],
            nx_recv.at[q],
            section=s + 1,
        ).start()

    def hand_on(n):
        @pl.when(jnp.logical_not(odd))
        def _():
            relay_ready(st_buf, x_buf, n, nx_send, ag_recv, section=s + 1)

        @pl.when(odd & (s < S - 1))
        def _():
            next_piece(start_order[n])

        @pl.when(s == S - 1)
        def _():
            relay_ready(st_buf, st_buf, n, sg_send, sg_recv)

    def output():
        project_out(0, middle)
        for k in range(pieces // 2):
            for way in (0, 1):
                emit(way, k, part[0, part_rows(piece_of(way, k)), :])
        for m in range(middle - 1, 0, -1):
            project_out(0, m)
            project_out(1, -m)
            for k in arrival_order:
                for way in (0, 1):
                    value = part[way, part_rows(piece_of(way, k)), :]
                    emit(way, slot_of(m, k), value + contribution(m, way, k))
        project_out(0, 0)
        for n, q in enumerate(start_order):
            place = part_rows(q)
            total = x_buf[z, place, :].astype(F32) + part[0, place, :]
            for way in (0, 1):
                total += contribution(0, way, piece_of(way, q))
            st_buf[z, place, :] = total.astype(BF16)
            hand_on(n)

    def hand_over():
        @pl.when(odd)
        def _():
            @pl.when(s < S - 1)
            def _():
                wait_bytes(x_buf.at[0], nx_send.at[0])
                for n in range(pieces):
                    relay_ready(st_buf, st_buf, n, sg_send, sg_recv)

            mate_copy(middle)

        send_state()

        @pl.when(jnp.logical_not(odd))
        def _():
            for q in range(pieces):
                next_piece(q)

    def send_state():
        for k in range(1, N):
            t = wrap(i + k)
            remote(
                st_buf.at[z, rows(t)], y_mid.at[i], m_send.at[0], m_recv.at[0], dp=t
            ).start()
        y_mid[i] = st_buf[z, rows(i), :]

    def pass_state():
        wait_bytes(y_mid.at[pl.ds(0, N - 1)], m_recv.at[0])
        for k in range(1, N):
            w = wrap(z + k)
            remote(
                y_mid.at[w], y_buf.at[rows(z)], y_send.at[0], y_recv.at[0], cand=w
            ).start()
        y_buf[rows(z), :] = y_mid[z]

    farthest = wrap(z + middle)

    def candidate(block, last=False):
        hidden = a_buf[block, :, pl.ds(QW, LANES)]
        branch = jnp.dot(hidden, w_up[...], preferred_element_type=F32)
        difference = branch - (st_buf[block].astype(F32) - x_buf[block].astype(F32))
        scaled = (difference * (1.0 / token_total)).astype(BF16)
        sc_buf[block] = scaled
        backward = dot_nt(scaled, w_up[...]).astype(BF16)
        if last:
            last_send[...] = backward
            for k in range(1, N):
                remote(
                    last_send, last_recv.at[i], d_send.at[0], d_recv.at[0], dp=wrap(i + k)
                ).start()
            last_recv[i] = backward
            return
        bw_send[block] = backward

        @pl.when(block == i)
        def _():
            bw_recv[i] = bw_send[block]

        @pl.when(block != i)
        def _():
            remote(
                bw_send.at[block], bw_recv.at[i], b_send.at[0], b_recv.at[0], dp=block
            ).start()

    def candidates():
        @pl.when(jnp.logical_not(odd))
        def _():
            wait_bytes(st_buf.at[wrap(z + middle)], mate_recv.at[middle])

        candidate(z)
        for j in range(middle):
            last = j == middle - 1

            @pl.when(odd)
            def _(j=j):
                for k in range(j * pieces, min((j + 1) * pieces, messages)):
                    gather_step(st_buf, k, sg_send, sg_recv)

            @pl.when(jnp.logical_not(odd))
            def _(j=j, last=last):
                if not last:
                    wait_bytes(st_buf.at[wrap(z + j + 1)], mate_recv.at[j + 1])
                    wait_bytes(st_buf.at[wrap(z - j - 1)], mate_recv.at[N - j - 1])

            candidate(wrap(z + j + 1), last)
            if not last:
                candidate(wrap(z - j - 1))


    def gradients():
        def finish(block, received):
            backward = received[0].astype(F32)
            for source in range(1, N):
                backward += received[source].astype(F32)
            extra = a_buf[block, :, pl.ds(QW, LANES)].astype(F32)
            inverse = extra[:, R : R + 1] + extra[:, R + 1 : R + 2]
            bw_all[block] = (backward * keep * inverse).astype(BF16)

        @pl.when(i != farthest)
        def _():
            wait_bytes(bw_recv.at[pl.ds(0, N - 1)], b_recv.at[0])
            finish(i, bw_recv)
            for k in range(1, N):
                remote(
                    bw_all.at[i], bw_all.at[i], c_send.at[0], c_recv.at[0], dp=wrap(i + k)
                ).start()

        hidden_all = a_buf[:, :, pl.ds(QW, LANES)].reshape(N * T, LANES)
        g_up[...] = dot_tn(hidden_all, sc_buf[...].reshape(N * T, F))
        up_copy = pltpu.make_async_copy(g_up.at[pl.ds(0, R)], up_out.at[0, 0], load_sem.at[0])
        up_copy.start()
        pass_state()

        wait_bytes(last_recv.at[pl.ds(0, N - 1)], d_recv.at[0])
        finish(farthest, last_recv)

        @pl.when(i != farthest)
        def _():
            wait_bytes(bw_all.at[pl.ds(0, N - 2)], c_recv.at[0])

        @pl.when(i == farthest)
        def _():
            wait_bytes(bw_all.at[pl.ds(0, N - 1)], c_recv.at[0])

        g_down[...] = (
            dot_tn(bw_all[...].reshape(N * T, LANES), x_buf[...].reshape(N * T, F)) * cg[...]
        )
        down_copy = pltpu.make_async_copy(
            g_down.at[pl.ds(0, R)], down_out.at[0, 0], load_sem.at[2]
        )
        down_copy.start()
        wait_bytes(y_buf.at[pl.ds(0, T - piece)], y_recv.at[0])
        y_copy = pltpu.make_async_copy(y_buf, states_out.at[0], load_sem.at[1])
        y_copy.start()
        up_copy.wait()
        y_copy.wait()
        down_copy.wait()

    def drain():
        @pl.when(s == 0)
        def _():
            wait_pieces_sent(in_send.at[0])

        others = pl.ds(0, N - 1)

        @pl.when(jnp.logical_not(odd))
        def _():
            wait_bytes(x_buf.at[others], ag_send.at[0])
            wait_bytes(x_buf.at[pl.ds(0, 3)], nx_send.at[0])

        @pl.when(odd)
        def _():
            wait_bytes(x_buf.at[pl.ds(0, N - 3)], ag_send.at[0])
            wait_bytes(st_buf.at[others], sg_send.at[0])
            wait_bytes(st_buf.at[others], mate_send.at[0])

        wait_bytes(p_buf.at[others], p_send.at[0])
        wait_bytes(a_buf.at[others], a_send.at[0])
        wait_bytes(s_send, rs_send.at[0])
        wait_bytes(y_mid.at[others], m_send.at[0])
        wait_bytes(y_mid.at[others], y_send.at[0])
        wait_bytes(last_recv.at[others], d_send.at[0])

        @pl.when(i != farthest)
        def _():
            wait_bytes(bw_send.at[pl.ds(0, N - 2)], b_send.at[0])
            wait_bytes(bw_all.at[others], c_send.at[0])

        @pl.when(i == farthest)
        def _():
            wait_bytes(bw_send.at[others], b_send.at[0])

    @pl.when(s == 0)
    def _():
        send_input()

    prepare()
    gather_and_project()
    attention()
    output()
    hand_over()
    candidates()
    gradients()
    drain()


def shards(
    inputs,
    parent_gain,
    query_weight,
    key_value_weight,
    output_weight,
    candidate_gain,
    candidate_down,
    candidate_up,
    kept_ranks,
):
    N = lax.axis_size("cand")
    S = lax.axis_size("section")
    T, F = inputs.shape
    R = candidate_down.shape[2]
    QW = query_weight.shape[2]
    KW = QW + 2 * HD
    pieces = PIECES
    messages = (N - 1) * pieces // 2
    sharing = N // (key_value_weight.shape[3] // HD)
    cos_table, sin_table = rope_tables(T)
    anywhere = pl.BlockSpec(memory_space=pl.ANY)
    dma = pltpu.SemaphoreType.DMA
    return pl.pallas_call(
        functools.partial(body, N, S, sharing),
        out_shape=(
            jax.ShapeDtypeStruct((1, T, F), BF16),
            jax.ShapeDtypeStruct((1, 1, R, F), F32),
            jax.ShapeDtypeStruct((1, 1, R, F), F32),
        ),
        in_specs=[anywhere] * 8 + [pl.BlockSpec(memory_space=pltpu.SMEM)] + [anywhere] * 2,
        out_specs=(anywhere,) * 3,
        scratch_shapes=[
            pltpu.VMEM((N, T, F), BF16),
            pltpu.VMEM((N, T, F), BF16),
            pltpu.VMEM((N, T, F), BF16),
            pltpu.VMEM((N, T, KW + LANES), BF16),
            pltpu.VMEM((N, T, KW + LANES), BF16),
            pltpu.VMEM((T, QW + LANES), BF16),
            pltpu.VMEM((N, T, QW + LANES), BF16),
            pltpu.VMEM((2, messages, T // pieces, F), BF16),
            pltpu.VMEM((2, messages, T // pieces, F), BF16),
            pltpu.VMEM((2, T, F), F32),
            pltpu.VMEM((F, KW), BF16),
            pltpu.VMEM((QW, F), BF16),
            pltpu.VMEM((LANES, F), BF16),
            pltpu.VMEM((LANES, F), BF16),
            pltpu.VMEM((1, F), F32),
            pltpu.VMEM((1, F), F32),
            pltpu.VMEM((T, HD), F32),
            pltpu.VMEM((T, HD), F32),
            pltpu.VMEM((N, T, LANES), BF16),
            pltpu.VMEM((N, T, LANES), BF16),
            pltpu.VMEM((N, T, LANES), BF16),
            pltpu.VMEM((T, LANES), BF16),
            pltpu.VMEM((N, T, LANES), BF16),
            pltpu.VMEM((N, T // N, F), BF16),
            pltpu.VMEM((T, F), BF16),
            pltpu.VMEM((LANES, F), F32),
            pltpu.VMEM((LANES, F), F32),
            dma((10,)),
            dma((1,)),
            dma((1,)),
            dma((1,)),
            dma((pieces,)),
            dma((1,)),
            dma((2, messages)),
            dma((1,)),
            dma((2, messages)),
            dma((1,)),
            dma((1,)),
            dma((1,)),
            dma((N,)),
            dma((1,)),
            dma((2, messages)),
            dma((1,)),
            dma((N,)),
            dma((1,)),
            dma((1,)),
            dma((1,)),
            dma((1,)),
            dma((1,)),
            dma((1,)),
            dma((1,)),
            dma((1,)),
            dma((1,)),
            dma((1,)),
        ],
        compiler_params=pltpu.CompilerParams(
            collective_id=0, has_side_effects=True, vmem_limit_bytes=56 * 1024 * 1024
        ),
    )(
        inputs,
        parent_gain,
        query_weight,
        key_value_weight,
        output_weight,
        candidate_gain,
        candidate_down,
        candidate_up,
        kept_ranks,
        jnp.asarray(cos_table),
        jnp.asarray(sin_table),
    )


def solution(mesh):
    placed = (
        P("dp", "cand"),
        P("section", None),
        P("section", "dp", "cand"),
        P("section", None, "dp", None),
        P("section", "cand", "dp"),
        P("section", "cand", None),
        P("section", "cand", None, None),
        P("section", "cand", None, None),
        P("section", "cand"),
    )
    return jax.shard_map(
        shards,
        mesh=mesh,
        in_specs=placed,
        out_specs=(
            P("section", "dp", "cand"),
            P("section", "cand", None, "dp"),
            P("section", "cand", None, "dp"),
        ),
        check_vma=False,
    )
```

```python
import functools

import jax
import jax.numpy as jnp
import numpy as np
from jax import lax
from jax.experimental import pallas as pl
from jax.experimental.pallas import tpu as pltpu
from jax.sharding import PartitionSpec as P

HD = 128
LANES = 128
PIECES = 8
EPSILON = 1e-05
ROPE_BASE = 500000.0
MESH = pl.DeviceIdType.MESH
F32 = jnp.float32
BF16 = jnp.bfloat16


def dot_nt(a, b):
    return lax.dot_general(a, b, (((1,), (1,)), ((), ())), preferred_element_type=F32)


def dot_tn(a, b):
    return lax.dot_general(a, b, (((0,), (0,)), ((), ())), preferred_element_type=F32)


def rope_tables(tokens):
    half = HD // 2
    frequency = (ROPE_BASE ** (-np.arange(half, dtype=np.float64) / half)).astype(np.float32)
    angles = np.arange(tokens, dtype=np.float32)[:, None] * frequency[None, :]
    angles = angles.astype(np.float64)
    cosine, sine = np.cos(angles), np.sin(angles)
    full_cos = np.concatenate([cosine, cosine], axis=1).astype(np.float32)
    full_sin = np.concatenate([-sine, sine], axis=1).astype(np.float32)
    return full_cos, full_sin


def body(
    N,
    S,
    sharing,
    inputs,
    parent_gain,
    query_weight,
    key_value_weight,
    output_weight,
    candidate_gain,
    candidate_down,
    candidate_up,
    kept,
    cos_table,
    sin_table,
    states_out,
    down_out,
    up_out,
    x_buf,
    st_buf,
    sc_buf,
    p_buf,
    r_buf,
    a_own,
    a_buf,
    s_send,
    s_recv,
    part,
    w_qkv,
    w_out,
    w_down,
    w_up,
    pg,
    cg,
    cos_v,
    sin_v,
    bw_send,
    bw_recv,
    bw_all,
    last_send,
    last_recv,
    y_mid,
    y_buf,
    g_down,
    g_up,
    load_sem,
    in_send,
    in_recv,
    nx_send,
    nx_recv,
    ag_send,
    ag_recv,
    sg_send,
    sg_recv,
    p_send,
    p_recv,
    a_send,
    a_recv,
    rs_send,
    rs_recv,
    mate_send,
    mate_recv,
    y_send,
    y_recv,
    b_send,
    b_recv,
    c_send,
    c_recv,
    d_send,
    d_recv,
    m_send,
    m_recv,
):
    s = lax.axis_index("section")
    z = lax.axis_index("cand")
    i = lax.axis_index("dp")
    T, F = inputs.shape
    R = candidate_down.shape[2]
    D = N * F
    QW = query_weight.shape[2]
    heads = QW // HD
    KW = QW + 2 * HD
    piece = T // N
    token_total = T * N
    middle = N // 2

    def wrap(index):
        return lax.rem(index + 2 * N, N)

    def rows(index):
        return pl.ds(pl.multiple_of(index * piece, piece), piece)

    def remote(source, target, send, recv, **device):
        return pltpu.make_async_remote_copy(
            src_ref=source,
            dst_ref=target,
            send_sem=send,
            recv_sem=recv,
            device_id=device,
            device_id_type=MESH,
        )

    def wait_bytes(ref, sem):
        pltpu.make_async_copy(ref, ref, sem).wait()

    features = pl.ds(pl.multiple_of(i * F, F), F)
    kv_columns = pl.ds(pl.multiple_of((z // sharing) * HD, HD), HD)
    loads = [
        (query_weight.at[0], w_qkv.at[:, pl.ds(0, QW)]),
        (key_value_weight.at[0, 0, :, kv_columns], w_qkv.at[:, pl.ds(QW, HD)]),
        (key_value_weight.at[0, 1, :, kv_columns], w_qkv.at[:, pl.ds(QW + HD, HD)]),
        (output_weight.at[0], w_out),
        (candidate_down.at[0, 0, :, features], w_down.at[pl.ds(0, R)]),
        (candidate_up.at[0, 0, :, features], w_up.at[pl.ds(0, R)]),
        (parent_gain.at[:, features], pg),
        (candidate_gain.at[0, :, features], cg),
        (cos_table, cos_v),
        (sin_table, sin_v),
    ]
    copies = [
        pltpu.make_async_copy(source, target, load_sem.at[k])
        for k, (source, target) in enumerate(loads)
    ]
    for copy in copies:
        copy.start()

    barrier = pltpu.get_barrier_semaphore()

    def greet(**device):
        pl.semaphore_signal(barrier, inc=1, device_id=device, device_id_type=MESH)

    diagonal = i == z
    odd = lax.rem(s, 2) == 1
    for k in range(1, N):
        greet(cand=wrap(z + k))
        greet(dp=wrap(i + k))
    for w in range(N):

        @pl.when(jnp.logical_not(diagonal & (z == w)))
        def _(w=w):
            greet(dp=z, cand=w)
            greet(dp=w, cand=i)

    @pl.when(s > 0)
    def _():
        greet(section=s - 1)

    @pl.when(s < S - 1)
    def _():
        greet(section=s + 1)

    mate = s + 1 - 2 * lax.rem(s, 2)
    greet(section=mate, cand=wrap(z + 1))
    greet(section=mate, cand=wrap(z - 1))

    expected = (
        2
        + 2 * (N - 1)
        + 2 * N
        - 2 * diagonal.astype(jnp.int32)
        + (s > 0).astype(jnp.int32)
        + (s < S - 1).astype(jnp.int32)
    )
    pl.semaphore_wait(barrier, expected)

    pieces = PIECES
    messages = (N - 1) * pieces // 2
    piece_rows = T // pieces

    def part_rows(q):
        return pl.ds(q * piece_rows, piece_rows)

    def piece_of(way, k):
        return k % pieces if way == 0 else pieces - 1 - k % pieces

    def toward(way):
        return wrap(z + 1 - 2 * way)

    def send_input():
        for w in range(N):
            source = inputs.at[pl.ds(w * piece, piece)]
            target = x_buf.at[w, rows(i)]
            own = diagonal & (z == w)

            @pl.when(own)
            def _(source=source, target=target):
                pltpu.make_async_copy(source, target, in_recv.at[0]).start()

            @pl.when(jnp.logical_not(own))
            def _(source=source, target=target, w=w):
                remote(source, target, in_send.at[0], in_recv.at[0], dp=z, cand=w).start()

    def wait_pieces_sent(sem):
        @pl.when(diagonal)
        def _():
            wait_bytes(y_buf.at[pl.ds(0, T - piece)], sem)

        @pl.when(jnp.logical_not(diagonal))
        def _():
            wait_bytes(y_buf, sem)

    def prepare():
        for copy in copies:
            copy.wait()
        w_down[pl.ds(R, LANES - R), :] = jnp.zeros((LANES - R, F), BF16)
        w_up[pl.ds(R, LANES - R), :] = jnp.zeros((LANES - R, F), BF16)
        w_down[pl.ds(0, R), :] = (w_down[pl.ds(0, R), :].astype(F32) * cg[...]).astype(BF16)

    def relay(source, target, block, distance, way, k, send, recv, **device):
        place = part_rows(piece_of(way, k))
        if distance < middle - 1 or (distance == middle - 1 and k < pieces // 2):
            remote(
                source.at[block, place],
                target.at[block, place],
                send.at[0],
                recv.at[way, distance * pieces + k],
                cand=toward(way),
                **device,
            ).start()

    def gather_step(buffer, k, send, recv):
        distance = k // pieces + 1
        for way in (0, 1):
            block = wrap(z - distance + 2 * distance * way)
            wait_bytes(buffer.at[block, part_rows(piece_of(way, k))], recv.at[way, k])
            relay(buffer, buffer, block, distance, way, k % pieces, send, recv)

    start_order = []
    for q in range(pieces // 2):
        start_order += [q, pieces - 1 - q]
    ready = []
    for n in range(pieces):
        done = set(start_order[: n + 1])
        fresh = []
        for way in (0, 1):
            for k in range(pieces):
                before = all(piece_of(way, b) in done for b in range(k + 1))
                if before and not any((way, k) in earlier for earlier in ready):
                    fresh.append((way, k))
        ready.append(fresh)

    def relay_ready(source, target, n, send, recv, **device):
        for way, k in ready[n]:
            relay(source, target, z, 0, way, k, send, recv, **device)

    lane = lax.broadcasted_iota(jnp.int32, (T, LANES), 1)
    keep = (lax.broadcasted_iota(jnp.int32, (1, LANES), 1) < kept[0, 0]).astype(F32)

    def project(block):
        values = x_buf[block]
        wide = values.astype(F32)
        scaled = (wide * pg[...]).astype(BF16)
        p_buf[block, :, pl.ds(0, KW)] = jnp.dot(
            scaled, w_qkv[...], preferred_element_type=F32
        ).astype(BF16)
        hidden = dot_nt(values, w_down[...])
        squares = jnp.sum(wide * wide, axis=-1, keepdims=True)
        coarse = squares.astype(BF16).astype(F32)
        extra = jnp.where(lane == R, coarse, jnp.where(lane == R + 1, squares - coarse, hidden))
        p_buf[block, :, pl.ds(KW, LANES)] = extra.astype(BF16)
        for k in range(1, N):
            t = wrap(i + k)
            remote(
                p_buf.at[block, rows(t)],
                r_buf.at[i, rows(block)],
                p_send.at[0],
                p_recv.at[0],
                dp=t,
            ).start()
        r_buf[i, rows(block), :] = p_buf[block, rows(i), :]

    def mate_copy(d):
        place = wrap(z + d)
        remote(
            x_buf.at[place], st_buf.at[place], mate_send.at[0], mate_recv.at[d], section=s - 1
        ).start()

    def gather_and_project():
        @pl.when(s == 0)
        def _():
            wait_bytes(x_buf.at[z], in_recv.at[0])

        for n, q in enumerate(start_order):

            @pl.when(s > 0)
            def _(q=q):
                wait_bytes(x_buf.at[z, part_rows(q)], nx_recv.at[q])

            @pl.when(jnp.logical_not(odd))
            def _(n=n):
                relay_ready(x_buf, x_buf, n, ag_send, ag_recv)

        project(z)
        for j in range(middle):
            for k in range(j * pieces, min((j + 1) * pieces, messages)):
                gather_step(x_buf, k, ag_send, ag_recv)
            project(wrap(z + j + 1))
            if j < middle - 1:
                project(wrap(z - j - 1))


    def summed(b):
        total = r_buf[0, :, pl.ds(b * LANES, LANES)].astype(F32)
        for source in range(1, N):
            total += r_buf[source, :, pl.ds(b * LANES, LANES)].astype(F32)
        return total

    def rotated(matrix):
        return (matrix * cos_v[...] + pltpu.roll(matrix, HD // 2, 1) * sin_v[...]).astype(BF16)

    offsets = [middle]
    for m in range(middle - 1, 0, -1):
        offsets += [m, -m]
    offsets.append(0)

    def attention():
        wait_bytes(r_buf.at[pl.ds(0, N - 1)], p_recv.at[0])
        extra = summed(heads + 2)
        squares = extra[:, R : R + 1] + extra[:, R + 1 : R + 2]
        inverse = lax.rsqrt(squares / D + EPSILON)
        hidden = extra * inverse * keep
        inverse_coarse = inverse.astype(BF16).astype(F32)
        a_own[:, pl.ds(QW, LANES)] = jnp.where(
            lane == R, inverse_coarse, jnp.where(lane == R + 1, inverse - inverse_coarse, hidden)
        ).astype(BF16)
        keys = rotated(summed(heads) * inverse)
        values = (summed(heads + 1) * inverse).astype(BF16)
        allowed = lax.broadcasted_iota(jnp.int32, (T, T), 1) <= lax.broadcasted_iota(
            jnp.int32, (T, T), 0
        )
        for h in range(heads):
            queries = rotated(summed(h) * inverse)
            scores = dot_nt(queries, keys) * HD ** (-0.5)
            raised = jnp.where(allowed, jnp.exp(scores), 0.0)
            weights = (raised / jnp.sum(raised, axis=-1, keepdims=True)).astype(BF16)
            a_own[:, pl.ds(h * HD, HD)] = jnp.dot(
                weights, values, preferred_element_type=F32
            ).astype(BF16)
        for d, offset in enumerate(offsets):
            block = wrap(z + offset)
            for k in range(1, N):
                remote(
                    a_own.at[rows(block)],
                    a_buf.at[block, rows(i)],
                    a_send.at[0],
                    a_recv.at[d],
                    dp=wrap(i + k),
                ).start()
            a_buf[block, rows(i), :] = a_own[rows(block), :]

        @pl.when(odd)
        def _():
            for d in range(1, N):
                if d != middle:
                    mate_copy(d)

    def project_out(slot, offset):
        block = wrap(z + offset)
        wait_bytes(a_buf.at[block, pl.ds(0, T - piece)], a_recv.at[offsets.index(offset)])
        part[slot] = jnp.dot(
            a_buf[block, :, pl.ds(0, QW)], w_out[...], preferred_element_type=F32
        )

    def got(way, k):
        wait_bytes(s_recv.at[way, k], rs_recv.at[way, k])
        return s_recv[way, k].astype(F32)

    def slot_of(offset, k):
        return pieces // 2 + (middle - 1 - offset) * pieces + k

    def contribution(offset, way, k):
        if offset < middle - 1:
            return got(way, slot_of(offset + 1, k))
        return got(way, k) if k < pieces // 2 else 0.0

    def emit(way, slot, value):
        s_send[way, slot] = value.astype(BF16)
        remote(
            s_send.at[way, slot],
            s_recv.at[way, slot],
            rs_send.at[0],
            rs_recv.at[way, slot],
            cand=toward(way),
        ).start()

    arrival_order = list(range(pieces // 2, pieces)) + list(range(pieces // 2))

    def next_piece(q):
        remote(
            st_buf.at[z, part_rows(q)],
            x_buf.at[z, part_rows(q)],
            nx_send.at[0],
            nx_recv.at[q],
            section=s + 1,
        ).start()

    def hand_on(n):
        @pl.when(jnp.logical_not(odd))
        def _():
            relay_ready(st_buf, x_buf, n, nx_send, ag_recv, section=s + 1)

        @pl.when(odd & (s < S - 1))
        def _():
            next_piece(start_order[n])

        @pl.when(s == S - 1)
        def _():
            relay_ready(st_buf, st_buf, n, sg_send, sg_recv)

    def output():
        project_out(0, middle)
        for k in range(pieces // 2):
            for way in (0, 1):
                emit(way, k, part[0, part_rows(piece_of(way, k)), :])
        for m in range(middle - 1, 0, -1):
            project_out(0, m)
            project_out(1, -m)
            for k in arrival_order:
                for way in (0, 1):
                    value = part[way, part_rows(piece_of(way, k)), :]
                    emit(way, slot_of(m, k), value + contribution(m, way, k))
        project_out(0, 0)
        for n, q in enumerate(start_order):
            place = part_rows(q)
            total = x_buf[z, place, :].astype(F32) + part[0, place, :]
            for way in (0, 1):
                total += contribution(0, way, piece_of(way, q))
            st_buf[z, place, :] = total.astype(BF16)
            hand_on(n)

    def hand_over():
        @pl.when(odd)
        def _():
            @pl.when(s < S - 1)
            def _():
                wait_bytes(x_buf.at[0], nx_send.at[0])
                for n in range(pieces):
                    relay_ready(st_buf, st_buf, n, sg_send, sg_recv)

            mate_copy(middle)

        send_state()

        @pl.when(jnp.logical_not(odd))
        def _():
            for q in range(pieces):
                next_piece(q)

    def send_state():
        for k in range(1, N):
            t = wrap(i + k)
            remote(
                st_buf.at[z, rows(t)], y_mid.at[i], m_send.at[0], m_recv.at[0], dp=t
            ).start()
        y_mid[i] = st_buf[z, rows(i), :]

    def pass_state():
        wait_bytes(y_mid.at[pl.ds(0, N - 1)], m_recv.at[0])
        for k in range(1, N):
            w = wrap(z + k)
            remote(
                y_mid.at[w], y_buf.at[rows(z)], y_send.at[0], y_recv.at[0], cand=w
            ).start()
        y_buf[rows(z), :] = y_mid[z]

    farthest = wrap(z + middle)

    def candidate(block, last=False):
        hidden = a_buf[block, :, pl.ds(QW, LANES)]
        branch = jnp.dot(hidden, w_up[...], preferred_element_type=F32)
        difference = branch - (st_buf[block].astype(F32) - x_buf[block].astype(F32))
        scaled = (difference * (1.0 / token_total)).astype(BF16)
        sc_buf[block] = scaled
        backward = dot_nt(scaled, w_up[...]).astype(BF16)
        if last:
            last_send[...] = backward
            for k in range(1, N):
                remote(
                    last_send, last_recv.at[i], d_send.at[0], d_recv.at[0], dp=wrap(i + k)
                ).start()
            last_recv[i] = backward
            return
        bw_send[block] = backward

        @pl.when(block == i)
        def _():
            bw_recv[i] = bw_send[block]

        @pl.when(block != i)
        def _():
            remote(
                bw_send.at[block], bw_recv.at[i], b_send.at[0], b_recv.at[0], dp=block
            ).start()

    def candidates():
        @pl.when(jnp.logical_not(odd))
        def _():
            wait_bytes(st_buf.at[wrap(z + middle)], mate_recv.at[middle])

        candidate(z)
        for j in range(middle):
            last = j == middle - 1

            @pl.when(odd)
            def _(j=j):
                for k in range(j * pieces, min((j + 1) * pieces, messages)):
                    gather_step(st_buf, k, sg_send, sg_recv)

            @pl.when(jnp.logical_not(odd))
            def _(j=j, last=last):
                if not last:
                    wait_bytes(st_buf.at[wrap(z + j + 1)], mate_recv.at[j + 1])
                    wait_bytes(st_buf.at[wrap(z - j - 1)], mate_recv.at[N - j - 1])

            candidate(wrap(z + j + 1), last)
            if not last:
                candidate(wrap(z - j - 1))


    def gradients():
        def finish(block, received):
            backward = received[0].astype(F32)
            for source in range(1, N):
                backward += received[source].astype(F32)
            extra = a_buf[block, :, pl.ds(QW, LANES)].astype(F32)
            inverse = extra[:, R : R + 1] + extra[:, R + 1 : R + 2]
            bw_all[block] = (backward * keep * inverse).astype(BF16)

        @pl.when(i != farthest)
        def _():
            wait_bytes(bw_recv.at[pl.ds(0, N - 1)], b_recv.at[0])
            finish(i, bw_recv)
            for k in range(1, N):
                remote(
                    bw_all.at[i], bw_all.at[i], c_send.at[0], c_recv.at[0], dp=wrap(i + k)
                ).start()

        hidden_all = a_buf[:, :, pl.ds(QW, LANES)].reshape(N * T, LANES)
        g_up[...] = dot_tn(hidden_all, sc_buf[...].reshape(N * T, F))
        up_copy = pltpu.make_async_copy(g_up.at[pl.ds(0, R)], up_out.at[0, 0], load_sem.at[0])
        up_copy.start()
        pass_state()

        wait_bytes(last_recv.at[pl.ds(0, N - 1)], d_recv.at[0])
        finish(farthest, last_recv)

        @pl.when(i != farthest)
        def _():
            wait_bytes(bw_all.at[pl.ds(0, N - 2)], c_recv.at[0])

        @pl.when(i == farthest)
        def _():
            wait_bytes(bw_all.at[pl.ds(0, N - 1)], c_recv.at[0])

        g_down[...] = (
            dot_tn(bw_all[...].reshape(N * T, LANES), x_buf[...].reshape(N * T, F)) * cg[...]
        )
        down_copy = pltpu.make_async_copy(
            g_down.at[pl.ds(0, R)], down_out.at[0, 0], load_sem.at[2]
        )
        down_copy.start()
        wait_bytes(y_buf.at[pl.ds(0, T - piece)], y_recv.at[0])
        y_copy = pltpu.make_async_copy(y_buf, states_out.at[0], load_sem.at[1])
        y_copy.start()
        up_copy.wait()
        y_copy.wait()
        down_copy.wait()

    def drain():
        @pl.when(s == 0)
        def _():
            wait_pieces_sent(in_send.at[0])

        others = pl.ds(0, N - 1)

        @pl.when(jnp.logical_not(odd))
        def _():
            wait_bytes(x_buf.at[others], ag_send.at[0])
            wait_bytes(x_buf.at[pl.ds(0, 3)], nx_send.at[0])

        @pl.when(odd)
        def _():
            wait_bytes(x_buf.at[pl.ds(0, N - 3)], ag_send.at[0])
            wait_bytes(st_buf.at[others], sg_send.at[0])
            wait_bytes(st_buf.at[others], mate_send.at[0])

        wait_bytes(p_buf.at[others], p_send.at[0])
        wait_bytes(a_buf.at[others], a_send.at[0])
        wait_bytes(s_send, rs_send.at[0])
        wait_bytes(y_mid.at[others], m_send.at[0])
        wait_bytes(y_mid.at[others], y_send.at[0])
        wait_bytes(last_recv.at[others], d_send.at[0])

        @pl.when(i != farthest)
        def _():
            wait_bytes(bw_send.at[pl.ds(0, N - 2)], b_send.at[0])
            wait_bytes(bw_all.at[others], c_send.at[0])

        @pl.when(i == farthest)
        def _():
            wait_bytes(bw_send.at[others], b_send.at[0])

    @pl.when(s == 0)
    def _():
        send_input()

    prepare()
    gather_and_project()
    attention()
    output()
    hand_over()
    candidates()
    gradients()
    drain()


def shards(
    inputs,
    parent_gain,
    query_weight,
    key_value_weight,
    output_weight,
    candidate_gain,
    candidate_down,
    candidate_up,
    kept_ranks,
):
    N = lax.axis_size("cand")
    S = lax.axis_size("section")
    T, F = inputs.shape
    R = candidate_down.shape[2]
    QW = query_weight.shape[2]
    KW = QW + 2 * HD
    pieces = PIECES
    messages = (N - 1) * pieces // 2
    sharing = N // (key_value_weight.shape[3] // HD)
    cos_table, sin_table = rope_tables(T)
    anywhere = pl.BlockSpec(memory_space=pl.ANY)
    dma = pltpu.SemaphoreType.DMA
    return pl.pallas_call(
        functools.partial(body, N, S, sharing),
        out_shape=(
            jax.ShapeDtypeStruct((1, T, F), BF16),
            jax.ShapeDtypeStruct((1, 1, R, F), F32),
            jax.ShapeDtypeStruct((1, 1, R, F), F32),
        ),
        in_specs=[anywhere] * 8 + [pl.BlockSpec(memory_space=pltpu.SMEM)] + [anywhere] * 2,
        out_specs=(anywhere,) * 3,
        scratch_shapes=[
            pltpu.VMEM((N, T, F), BF16),
            pltpu.VMEM((N, T, F), BF16),
            pltpu.VMEM((N, T, F), BF16),
            pltpu.VMEM((N, T, KW + LANES), BF16),
            pltpu.VMEM((N, T, KW + LANES), BF16),
            pltpu.VMEM((T, QW + LANES), BF16),
            pltpu.VMEM((N, T, QW + LANES), BF16),
            pltpu.VMEM((2, messages, T // pieces, F), BF16),
            pltpu.VMEM((2, messages, T // pieces, F), BF16),
            pltpu.VMEM((2, T, F), F32),
            pltpu.VMEM((F, KW), BF16),
            pltpu.VMEM((QW, F), BF16),
            pltpu.VMEM((LANES, F), BF16),
            pltpu.VMEM((LANES, F), BF16),
            pltpu.VMEM((1, F), F32),
            pltpu.VMEM((1, F), F32),
            pltpu.VMEM((T, HD), F32),
            pltpu.VMEM((T, HD), F32),
            pltpu.VMEM((N, T, LANES), BF16),
            pltpu.VMEM((N, T, LANES), BF16),
            pltpu.VMEM((N, T, LANES), BF16),
            pltpu.VMEM((T, LANES), BF16),
            pltpu.VMEM((N, T, LANES), BF16),
            pltpu.VMEM((N, T // N, F), BF16),
            pltpu.VMEM((T, F), BF16),
            pltpu.VMEM((LANES, F), F32),
            pltpu.VMEM((LANES, F), F32),
            dma((10,)),
            dma((1,)),
            dma((1,)),
            dma((1,)),
            dma((pieces,)),
            dma((1,)),
            dma((2, messages)),
            dma((1,)),
            dma((2, messages)),
            dma((1,)),
            dma((1,)),
            dma((1,)),
            dma((N,)),
            dma((1,)),
            dma((2, messages)),
            dma((1,)),
            dma((N,)),
            dma((1,)),
            dma((1,)),
            dma((1,)),
            dma((1,)),
            dma((1,)),
            dma((1,)),
            dma((1,)),
            dma((1,)),
            dma((1,)),
            dma((1,)),
        ],
        compiler_params=pltpu.CompilerParams(
            collective_id=0, has_side_effects=True, vmem_limit_bytes=56 * 1024 * 1024
        ),
    )(
        inputs,
        parent_gain,
        query_weight,
        key_value_weight,
        output_weight,
        candidate_gain,
        candidate_down,
        candidate_up,
        kept_ranks,
        jnp.asarray(cos_table),
        jnp.asarray(sin_table),
    )


def solution(mesh):
    placed = (
        P("dp", "cand"),
        P("section", None),
        P("section", "dp", "cand"),
        P("section", None, "dp", None),
        P("section", "cand", "dp"),
        P("section", "cand", None),
        P("section", "cand", None, None),
        P("section", "cand", None, None),
        P("section", "cand"),
    )
    return jax.shard_map(
        shards,
        mesh=mesh,
        in_specs=placed,
        out_specs=(
            P("section", "dp", "cand"),
            P("section", "cand", None, "dp"),
            P("section", "cand", None, "dp"),
        ),
        check_vma=False,
    )
```
